32 devices in a mesh: group: 2 (over y), ctx: 4 (over z), head: 4 (over x, core).
Axes of the slice: x: 2, y: 2, z: 4, core: 2. Of those that a mesh axis runs over, the one named last changes fastest.
Arguments:
- query: bfloat16 [1024, 4096], P(('group', 'ctx'), 'head'), parts along dimension 0, may hold values from -8 to 8
- keys: bfloat16 [1024, 512], P(('group', 'ctx'), 'head'), parts along dimension 0, may hold values from -6 to 6
- values: bfloat16 [1024, 512], P(('group', 'ctx'), 'head'), parts along dimension 0, may hold values from -6 to 6
- residual: bfloat16 [1024, 2048], P(('group', 'ctx', 'head')), parts along dimension 0, may hold values from -15 to 15
- o_weight: bfloat16 [4096, 2048], P('head', 'ctx'), may hold values from -0.09375 to 0.09375
- gain: float32 [2048], replicated, may hold values from 0.1 to 1.9
- routes: int32 [1024, 8], P(('group', 'ctx', 'head')), parts along dimension 0, may hold values from 0 to 15, all different within a row; in each aligned block of 32 rows (0 to 31, 32 to 63, ...) at most 32 rows name the same one
- gates: float32 [1024, 8], P(('group', 'ctx', 'head')), parts along dimension 0, may hold values from 0.05 to 1
- w_gate: bfloat16 [16, 2048, 768], P(('ctx', 'head')), may hold values from -0.125 to 0.125
- w_up: bfloat16 [16, 2048, 768], P(('ctx', 'head')), may hold values from -0.125 to 0.125
- w_down: bfloat16 [16, 768, 2048], P(('ctx', 'head')), may hold values from -0.625 to 0.625
Outputs:
- mixed: bfloat16 [1024, 2048], P(('group', 'ctx', 'head')), parts along dimension 0
- expert_mix: bfloat16 [1024, 2048], P(('group', 'ctx', 'head')), parts along dimension 0
The draws below stay inside these ranges and needn't reach their ends.
There are 2 independent parts, one for each index of `group`. The reference program is written for one: setup_inputs(seed, part) draws one part's arguments, and reference() takes and returns one part's arrays. A program takes and returns all parts, laid end to end along the dimension named above; an argument that names none is the same for every part. Nothing has to cross between parts.
Inputs may be any that keep to these rules, and one draw needn't show every extreme that they name: `routes`: the 8 experts of a token are distinct. In each aligned block of 32 tokens (the tokens of one owner device), no expert is named more than 32 times, a bound that some block reaches.
All inputs are finite; a program needn't handle non-finite values.
Results may differ from the reference program's by a relative error of at most 0.019.
Values may be sent and summed in bfloat16 or wider, within the bound.
A program may use at most 128 MiB of HBM per device.

```python
import math
import jax
import jax.numpy as jnp
import numpy as np
from jax import lax

D = 2048
QUERY_HEADS = 32
KEY_VALUE_HEADS = 4
HEAD_DIMENSION = 128
FE = 768
TOPK = 8
PROMPT_TOKENS = 512
TOK_OWN = 32
EXPERTS = 16
CAP = 32
N_CTX = 4
N_HEAD = 4


def draw_query(key, part):
    random_seed_key = jax.random.fold_in(key, 11)
    return jnp.clip(2.5 * jax.random.normal(random_seed_key, (PROMPT_TOKENS, QUERY_HEADS * HEAD_DIMENSION), jnp.float32), -8.0, 8.0).astype(jnp.bfloat16)


def draw_keys(key, part):
    random_seed_key = jax.random.fold_in(key, 23)
    return jnp.clip(jax.random.normal(random_seed_key, (PROMPT_TOKENS, KEY_VALUE_HEADS * HEAD_DIMENSION), jnp.float32), -6.0, 6.0).astype(jnp.bfloat16)


def draw_residual(key, part):
    row_key = jax.random.fold_in(key, 31)
    col_key = jax.random.fold_in(key, 37)
    random_seed_key = jax.random.fold_in(key, 41)
    row_scale = jnp.exp(jax.random.uniform(row_key, (PROMPT_TOKENS, 1), jnp.float32, jnp.log(0.3), jnp.log(1.5)))
    col_scale = jnp.exp(jax.random.uniform(col_key, (1, D), jnp.float32, jnp.log(0.25), jnp.log(2.5)))
    random_field = jnp.clip(jax.random.normal(random_seed_key, (PROMPT_TOKENS, D), jnp.float32), -4.0, 4.0)
    return (random_field * row_scale * col_scale).astype(jnp.bfloat16)


def block_levels(stream_key, shape, split, least, largest):
    factor_of, own = 1.0, jax.random.fold_in(stream_key, 6)
    for axis_at, blocks in split:
        steps = jnp.exp(jax.random.uniform(jax.random.fold_in(own, axis_at), (blocks,), jnp.float32, least / len(split), largest / len(split)))
        factor_of = factor_of * jnp.repeat(steps, shape[axis_at] // blocks).reshape([-1 if axis == axis_at else 1 for axis in range(len(shape))])
    return factor_of


def shared_out(own_key, own, number, rows, number_of, top, limit, skew):
    ranking = jax.random.permutation(own_key, number_of)
    heavy_load, usual = portions_of(number_of, rows * top, limit, skew, True), portions_of(number_of, rows * top, limit, skew, False)
    places = jnp.arange(number_of)

    def named(sizes, turn):
        used = int((sizes > 0).sum())
        fixed = max(1, used // 4)
        moved = fixed + (places - fixed + turn * (used - fixed)) % max(1, number_of - fixed)
        return jnp.zeros((number_of,), jnp.int32).at[ranking[jnp.where(places < fixed, places, moved)]].set(jnp.asarray(sizes, jnp.int32))

    sizes = jnp.where(number % 4 == 0, named(heavy_load, number // 4), named(usual, number - number // 4 - 1))
    mixed = jax.random.permutation(jax.random.fold_in(own, 3), number_of)
    giver, sink = mixed[0:number_of // 2 * 2:2], mixed[1:number_of // 2 * 2:2]
    margin = jnp.minimum(sizes[giver] - 1, limit - sizes[sink]) // 2
    margin = jnp.where((giver == ranking[0]) | (sink == ranking[0]) | (sizes[sink] == 0), 0, jnp.maximum(margin, 0))
    moved = jax.random.randint(jax.random.fold_in(own, 4), (number_of // 2,), 0, 1 << 20) % (margin + 1)
    sizes = sizes.at[giver].add(-moved).at[sink].add(moved)
    labels = jnp.searchsorted(jnp.cumsum(sizes), jnp.arange(rows * top), side="right").astype(jnp.int32)
    listing = labels.reshape(top, rows).T
    listing = listing[jax.random.permutation(jax.random.fold_in(own, 1), rows)]
    turn = jax.random.randint(jax.random.fold_in(own, 2), (rows, 1), 0, top)
    return jnp.take_along_axis(listing, (jnp.arange(top)[None, :] + turn) % top, axis=1)


def portions_of(number_of, total, limit, slope, full):
    portions = [(1 << 20) // math.isqrt(grade ** slope) + 1 for grade in range(1, number_of + 1)]
    largest = limit if full else min(limit, max(-(-total // number_of), total * portions[0] // sum(portions)))
    least = 1 if total - largest >= number_of - 1 else 0
    holding, spare = [largest] + [least] * (number_of - 1), total - largest - least * (number_of - 1)
    while spare > 0:
        movable = [i for i in range(1, number_of) if holding[i] < largest] or [i for i in range(1, number_of) if holding[i] < limit]
        mass, budget = sum([portions[i] for i in movable]), spare
        for i in movable:
            extra = min(limit - holding[i], max(1, budget * portions[i] // mass), spare)
            holding[i] = holding[i] + extra
            spare = spare - extra
    return np.array(holding)


def noise(own_key, shape, scale, limit, pieces=(), kind=jnp.bfloat16):
    drawn = scale * jax.random.normal(own_key, shape, jnp.float32)
    if pieces:
        drawn = drawn * block_levels(own_key, shape, pieces, -0.22, 0.18)
    return jnp.clip(drawn, -limit, limit).astype(kind)


def setup_inputs(seed: int = 0, part: int = 0) -> dict:
    key_of = jax.random.split(jax.random.key(seed), 12)
    part_splits = jax.random.split(jax.random.fold_in(key_of[11], part), 12)
    query = draw_query(jax.random.fold_in(jax.random.fold_in(key_of[11], part), 71), part)
    keys = draw_keys(jax.random.fold_in(jax.random.fold_in(key_of[11], part), 71), part)
    values = noise(part_splits[2], (PROMPT_TOKENS, KEY_VALUE_HEADS * HEAD_DIMENSION), 1.0, 6.0, ((0, 4), (1, 4)))
    residual = draw_residual(jax.random.fold_in(jax.random.fold_in(key_of[11], part), 71), part)
    o_weight = noise(key_of[4], (QUERY_HEADS * HEAD_DIMENSION, D), (QUERY_HEADS * HEAD_DIMENSION) ** -0.5, 0.09375, ((0, 4), (1, 4)))
    gain = jnp.clip(1.0 + 0.18 * jax.random.normal(key_of[5], (D,), jnp.float32), 0.1, 1.9)
    routes_keys = jax.random.split(jax.random.fold_in(part_splits[6], 1), PROMPT_TOKENS // TOK_OWN)
    routes_turns = jax.random.permutation(jax.random.fold_in(part_splits[6], 3), PROMPT_TOKENS // TOK_OWN)
    routes = jax.vmap(lambda own, number: shared_out(jax.random.fold_in(part_splits[6], 2), own, number, TOK_OWN, EXPERTS, TOPK, CAP, 2))(routes_keys, routes_turns).reshape((PROMPT_TOKENS, TOPK))
    gates = jnp.clip(jnp.exp(math.log(1.0) - 2.9957323 * jax.random.uniform(part_splits[7], (PROMPT_TOKENS, TOPK), jnp.float32) ** block_levels(part_splits[7], (PROMPT_TOKENS, TOPK), ((0, 16),), -0.2, 0.2)), 0.05, 1.0)
    w_gate = noise(key_of[8], (EXPERTS, D, FE), D ** -0.5, 0.125, ((0, 16),))
    w_up = noise(key_of[9], (EXPERTS, D, FE), D ** -0.5, 0.125, ((0, 16),))
    w_down = noise(key_of[10], (EXPERTS, FE, D), (FE // 8) ** -0.5, 0.625, ((0, 16),))
    return dict(query=query, keys=keys, values=values, residual=residual, o_weight=o_weight, gain=gain, routes=routes, gates=gates, w_gate=w_gate, w_up=w_up, w_down=w_down)


def attend_one(operands):
    q_head, k_head, v_head = operands
    positions = jnp.arange(PROMPT_TOKENS, dtype=jnp.int32)
    causal = positions[None, :] <= positions[:, None]
    scores = jnp.dot(q_head, k_head.T, preferred_element_type=jnp.float32) * HEAD_DIMENSION ** (-0.5)
    scores = jnp.where(causal, scores, -1e+30)
    row_max = lax.optimization_barrier(jnp.max(scores, axis=-1, keepdims=True))
    expw = jnp.where(causal, jnp.exp(scores - row_max), 0.0)
    total = lax.optimization_barrier(jnp.sum(expw, axis=-1, keepdims=True))
    summed = jnp.dot(expw.astype(jnp.bfloat16), v_head, preferred_element_type=jnp.float32)
    return (summed / total).astype(jnp.bfloat16)

def reference(query, keys, values, residual, o_weight, gain, routes, gates, w_gate, w_up, w_down):
    head_replicas = QUERY_HEADS // KEY_VALUE_HEADS
    selector_index = jnp.arange(QUERY_HEADS, dtype=jnp.int32) // head_replicas
    q_heads = query.reshape(PROMPT_TOKENS, QUERY_HEADS, HEAD_DIMENSION).transpose(1, 0, 2)
    key_head_tensor = keys.reshape(PROMPT_TOKENS, KEY_VALUE_HEADS, HEAD_DIMENSION).transpose(1, 0, 2)[selector_index]
    value_head_tensor = values.reshape(PROMPT_TOKENS, KEY_VALUE_HEADS, HEAD_DIMENSION).transpose(1, 0, 2)[selector_index]
    attended = lax.map(attend_one, (q_heads, key_head_tensor, value_head_tensor))
    attended = attended.transpose(1, 0, 2).reshape(PROMPT_TOKENS, QUERY_HEADS * HEAD_DIMENSION)
    projected = jnp.dot(attended, o_weight, preferred_element_type=jnp.float32)
    mixed = (projected + residual.astype(jnp.float32)).astype(jnp.bfloat16)
    mixed_f = mixed.astype(jnp.float32)
    normed = (mixed_f * lax.rsqrt(lax.optimization_barrier(jnp.mean(mixed_f * mixed_f, axis=-1, keepdims=True)) + 1e-06) * gain).astype(jnp.bfloat16)
    sources = N_CTX * N_HEAD
    expert_ids = routes.reshape(sources, TOK_OWN * TOPK)
    onehot = (expert_ids[..., None] == jnp.arange(EXPERTS, dtype=jnp.int32)).astype(jnp.int32)
    slots = lax.optimization_barrier(jnp.sum((jnp.cumsum(onehot, axis=1) - 1) * onehot, axis=-1)).astype(jnp.int32)
    token_ids = (jnp.arange(PROMPT_TOKENS * TOPK, dtype=jnp.int32) // TOPK).reshape(sources, TOK_OWN * TOPK)
    source_ids = jnp.arange(sources, dtype=jnp.int32)[:, None]
    columns = (source_ids * CAP + slots).astype(jnp.int32)
    weight_norm = gates / lax.optimization_barrier(jnp.sum(gates, axis=-1, keepdims=True))
    table = jnp.full((EXPERTS, sources * CAP), PROMPT_TOKENS, dtype=jnp.int32).at[expert_ids, columns].set(token_ids)
    weight_table = jnp.zeros((EXPERTS, sources * CAP), jnp.float32).at[expert_ids, columns].set(weight_norm.reshape(sources, -1))
    padded = jnp.concatenate([normed, jnp.zeros((1, D), jnp.bfloat16)], axis=0)

    def expert_step(running, operands):
        row_ids, row_weights, gate_proj, up_proj, down_proj = operands
        inputs = padded[row_ids]
        gate_act = jnp.dot(inputs, gate_proj, preferred_element_type=jnp.float32)
        up_act = jnp.dot(inputs, up_proj, preferred_element_type=jnp.float32)
        hidden = (jax.nn.silu(gate_act) * up_act).astype(jnp.bfloat16)
        output = jnp.dot(hidden, down_proj, preferred_element_type=jnp.float32).astype(jnp.bfloat16)
        return (running.at[row_ids].add(output.astype(jnp.float32) * row_weights[:, None]), None)
    running, _ = lax.scan(expert_step, jnp.zeros((PROMPT_TOKENS + 1, D), jnp.float32), (table, weight_table, w_gate, w_up, w_down))
    expert_mix = running[:PROMPT_TOKENS].astype(jnp.bfloat16)
    return (mixed, expert_mix)
```

```python
import jax
import jax.numpy as jnp
from jax import lax
from jax.experimental import pallas as pl
from jax.experimental.pallas import tpu as pltpu
from jax.sharding import PartitionSpec as P

HEAD_DIMENSION = 128


def expert_apply(arrived, gate_proj, up_proj, down_proj):
    shape_in = arrived.shape
    flat_rows = arrived.reshape(-1, shape_in[-1])
    gate_act = jnp.dot(flat_rows, gate_proj, preferred_element_type=jnp.float32)
    up_act = jnp.dot(flat_rows, up_proj, preferred_element_type=jnp.float32)
    hidden = (jax.nn.silu(gate_act) * up_act).astype(jnp.bfloat16)
    output = jnp.dot(hidden, down_proj, preferred_element_type=jnp.float32).astype(jnp.bfloat16)
    return output.reshape(shape_in)


def body(query, keys, values, residual, o_weight, gain, routes, gates, w_gate, w_up, w_down):
    head_size = HEAD_DIMENSION
    query_rows = query.shape[0]
    kv_heads = keys.shape[1] // head_size
    q_heads = query.shape[1] // head_size
    head_replicas = q_heads // kv_heads
    scale = head_size ** (-0.5)
    queries = query.reshape(query_rows, kv_heads, head_replicas, head_size)
    first_pos = lax.axis_index("ctx") * query_rows
    query_pos = first_pos + jnp.arange(query_rows, dtype=jnp.int32)
    last_pos = first_pos + query_rows - 1

    def accumulate(carry, pieces):
        run_max, run_sum, run_acc = carry
        key_piece, value_piece = pieces
        width = key_piece.shape[0]
        key_pos = jnp.arange(width, dtype=jnp.int32)
        visible = key_pos[None, :] <= query_pos[:, None]
        scores = (
            jnp.einsum(
                "veqi,zei->eqvz",
                queries,
                key_piece.reshape(width, kv_heads, head_size),
                preferred_element_type=jnp.float32,
            )
            * scale
        )
        scores = jnp.where(visible, scores, -1e30)
        new_max = jnp.maximum(run_max, jnp.max(scores, axis=-1))
        weights = jnp.where(visible, jnp.exp(scores - new_max[..., None]), 0.0)
        new_sum = jnp.sum(weights, axis=-1)
        update = jnp.einsum(
            "pexa,apo->pexo",
            weights.astype(jnp.bfloat16),
            value_piece.reshape(width, kv_heads, head_size),
            preferred_element_type=jnp.float32,
        )
        return (new_max, new_sum, update)

    start_state = (
        jnp.full((kv_heads, head_replicas, query_rows), -1e30, jnp.float32),
        jnp.zeros((kv_heads, head_replicas, query_rows), jnp.float32),
        jnp.zeros((kv_heads, head_replicas, query_rows, head_size), jnp.float32),
    )
    pieces = (
        lax.all_gather(keys, "ctx", axis=0, tiled=True),
        lax.all_gather(values, "ctx", axis=0, tiled=True),
    )
    run_max, run_sum, run_acc = lax.cond(
        jnp.int32(0) > last_pos, lambda: start_state, lambda: accumulate(start_state, pieces)
    )
    attended = (
        (run_acc / run_sum[..., None])
        .transpose(2, 0, 1, 3)
        .reshape(query_rows, q_heads * head_size)
        .astype(jnp.bfloat16)
    )
    head_terms = jnp.dot(
        attended,
        lax.all_gather(o_weight, "ctx", axis=1, tiled=True),
        preferred_element_type=jnp.float32,
    )
    summed = lax.psum_scatter(
        head_terms.astype(jnp.bfloat16), "head", scatter_dimension=0, tiled=True
    ).astype(jnp.float32)
    mixed = (summed + residual.astype(jnp.float32)).astype(jnp.bfloat16)
    mixed_f = mixed.astype(jnp.float32)
    normed = (
        mixed_f * lax.rsqrt(jnp.mean(mixed_f * mixed_f, axis=-1, keepdims=True) + 1e-06) * gain
    ).astype(jnp.bfloat16)
    own_rows = residual.shape[0]
    model_dim = residual.shape[1]
    top_count = routes.shape[1]
    ctx_count = lax.axis_size("ctx")
    head_count = lax.axis_size("head")
    devices = ctx_count * head_count
    capacity = min(own_rows, max(2, 2 * own_rows * top_count // devices))
    expert_ids = routes.reshape(-1)
    onehot = (expert_ids[:, None] == jnp.arange(devices, dtype=jnp.int32)[None, :]).astype(
        jnp.int32
    )
    slots = jnp.sum((jnp.cumsum(onehot, axis=0) - 1) * onehot, axis=1)
    target = expert_ids * capacity + slots
    outgoing = (
        jnp.zeros((devices * capacity, model_dim), jnp.bfloat16)
        .at[target]
        .set(jnp.repeat(normed, top_count, axis=0))
    )
    outgoing = outgoing.reshape(devices, capacity, model_dim)
    gate_proj = w_gate[0]
    up_proj = w_up[0]
    down_proj = w_down[0]
    computed = expert_apply(
        lax.all_to_all(outgoing, ("ctx", "head"), split_axis=0, concat_axis=0, tiled=True),
        gate_proj,
        up_proj,
        down_proj,
    )
    returned = lax.all_to_all(computed, ("ctx", "head"), split_axis=0, concat_axis=0, tiled=True)
    selected_entries = returned.reshape(devices * capacity, model_dim)[target]
    selected_entries = selected_entries.astype(jnp.float32).reshape(own_rows, top_count, model_dim)
    weight_norm = gates / jnp.sum(gates, axis=-1, keepdims=True)
    expert_mix = jnp.sum(selected_entries * weight_norm[..., None], axis=1).astype(jnp.bfloat16)
    return (mixed, expert_mix)


LANES = 128
PIECES = 2
MESH = pl.DeviceIdType.MESH


def layer_kernel(
    n_ctx,
    q_ref, k_ref, v_ref, res_ref, wo_hbm, gain_ref, routes_ref, gates_ref, wg_hbm, wu_hbm, wd_hbm,
    mixed_ref, out_ref,
    wo, wg, wu, wd,
    kv, att, part, part_in, cross, cross_in, proj,
    tok, epart, epart_in, ecross, ecross_in, back,
    local_sem,
    kv_s, kv_r, att_s, att_r, pa_s, pa_r, px_s, px_r, pz_s, pz_r,
    tz_s, tz_r, tx_s, tx_r, tc_s, tc_r, ea_s, ea_r, ex_s, ex_r, ez_s, ez_r,
):
    f32, bf16 = jnp.float32, jnp.bfloat16
    z = lax.axis_index("ctx")
    h = lax.axis_index("head")
    x, core = h // 2, h % 2
    core_peer = x * 2 + (1 - core)
    x_peer = (1 - x) * 2 + core
    rows, own, model = q_ref.shape[0], res_ref.shape[0], res_ref.shape[1]
    size = HEAD_DIMENSION
    q_heads = q_ref.shape[1] // size
    piece_heads = q_heads // PIECES
    piece_width = piece_heads * size
    block = model // n_ctx
    hidden = wg.shape[1]

    loads = [
        pltpu.make_async_copy(src, dst, local_sem.at[i])
        for i, (src, dst) in enumerate(
            ((wo_hbm, wo), (wg_hbm.at[0], wg), (wu_hbm.at[0], wu), (wd_hbm.at[0], wd))
        )
    ]
    for load in loads:
        load.start()

    barrier = pltpu.get_barrier_semaphore()
    for peer in (core_peer, x_peer):
        pl.semaphore_signal(barrier, inc=1, device_id={"head": peer}, device_id_type=MESH)
    for step in range(1, n_ctx):
        pl.semaphore_signal(
            barrier, inc=1, device_id={"ctx": (z + step) % n_ctx}, device_id_type=MESH
        )

    kv[z, 0] = k_ref[...]
    kv[z, 1] = v_ref[...]
    for other in range(1, n_ctx):

        @pl.when(z < other)
        def _():
            kv[other] = jnp.zeros(kv.shape[1:], bf16)

    gate_values = gates_ref[...]
    gate_norm = gate_values / jnp.sum(gate_values, axis=-1, keepdims=True)
    route_values = routes_ref[...]
    lane = lax.broadcasted_iota(jnp.int32, (own, LANES), 1)
    half = LANES // 2
    table = jnp.zeros((own, LANES), f32)
    for k in range(route_values.shape[1]):
        table = table + jnp.where(
            lane % half == route_values[:, k : k + 1], gate_norm[:, k : k + 1], 0.0
        )
    high = table.astype(bf16).astype(f32)
    tok[z, h, :, model:] = jnp.where(lane < half, high, table - high).astype(bf16)

    pl.semaphore_wait(barrier, n_ctx + 1)

    def to_ctx(src, dst, send, recv, target):
        return pltpu.make_async_remote_copy(
            src_ref=src, dst_ref=dst, send_sem=send, recv_sem=recv,
            device_id={"ctx": target}, device_id_type=MESH,
        )

    def to_head(src, dst, send, recv, target):
        return pltpu.make_async_remote_copy(
            src_ref=src, dst_ref=dst, send_sem=send, recv_sem=recv,
            device_id={"head": target}, device_id_type=MESH,
        )

    last = n_ctx - 1
    short = jnp.minimum(z, last - z)
    toward = jnp.where(z * 2 < last, -1, 1)

    def source(i):
        if i == 0:
            return z
        near = toward * ((i + 1) // 2) if i % 2 else -toward * (i // 2)
        return z + jnp.where(i <= 2 * short, near, -toward * (i - short))

    def kv_copy(s):
        return to_ctx(kv.at[s], kv.at[s], kv_s.at[s], kv_r.at[s], jnp.minimum(z + 1, last))

    @pl.when(z < last)
    def _():
        kv_copy(z).start()

    for step in range(1, n_ctx):

        @pl.when(z >= step)
        def _():
            s = z - step
            kv_copy(s).wait_recv()

            @pl.when(z < last)
            def _():
                kv_copy(s).start()

    def chain(buf_at, send, recv, s, go_right):
        way = 1 if go_right else 0
        target = jnp.clip(z + (1 if go_right else -1), 0, last)
        return to_ctx(buf_at, buf_at, send.at[way], recv, target)

    def chain_each(i, s, run):
        @pl.when((s <= z) & (z < last))
        def _():
            run(True)

        @pl.when((s >= z) & (z > 0))
        def _():
            run(False)

    def att_copy(s, p, go_right):
        return chain(att.at[s, p], att_s.at[s, p], att_r.at[s, p], s, go_right)

    keys_all = kv[:, 0].reshape(n_ctx * rows, size)
    values_all = kv[:, 1].reshape(n_ctx * rows, size)
    row_at = lax.broadcasted_iota(jnp.int32, (rows, n_ctx * rows), 0)
    col_at = lax.broadcasted_iota(jnp.int32, (rows, n_ctx * rows), 1)
    visible = col_at <= row_at + z * rows
    scale = size ** (-0.5)
    for p in range(PIECES):
        for j in range(piece_heads):
            head = p * piece_heads + j
            scores = lax.dot_general(
                q_ref[:, head * size : (head + 1) * size],
                keys_all,
                (((1,), (1,)), ((), ())),
                preferred_element_type=f32,
            )
            scores = jnp.where(visible, scores * scale, -1e30)
            top = jnp.max(scores, axis=-1, keepdims=True)
            weights = jnp.where(visible, jnp.exp(scores - top), 0.0)
            total = jnp.sum(weights, axis=-1, keepdims=True)
            summed = jnp.dot(weights.astype(bf16), values_all, preferred_element_type=f32)
            att[z, p, :, j * size : (j + 1) * size] = (summed / total).astype(bf16)
        chain_each(0, z, lambda right, p=p: att_copy(z, p, right).start())

    def swap_core(buf, buf_in, send, recv, i):
        return to_head(buf.at[i, 1 - core], buf_in.at[i], send.at[i], recv.at[i], core_peer)

    def swap_x(buf, buf_in, send, recv, i):
        return to_head(buf.at[i], buf_in.at[i], send.at[i], recv.at[i], x_peer)

    def to_owner(buf, dst, send, recv, i):
        return to_ctx(buf.at[i], dst.at[z], send.at[i], recv.at[z], source(i))

    def store_chunk(buf, i, columns, value):
        parts = value.astype(bf16).reshape(2, 2, own, value.shape[-1])
        for cc in range(2):
            for xx in range(2):
                buf[i, cc, xx, :, columns] = parts[xx, cc]

    def after_core(i, buf, buf_in, crossed, a_s, a_r, crossed_in, x_s, x_r):
        swap_core(buf, buf_in, a_s, a_r, i).wait_recv()
        crossed[i] = (
            buf[i, core, 1 - x].astype(f32) + buf_in[i, 1 - x].astype(f32)
        ).astype(bf16)
        swap_x(crossed, crossed_in, x_s, x_r, i).start()

    def after_x(i, buf, buf_in, crossed_in, crossed, x_s, x_r, dst, own_sum, z_s, z_r):
        swap_x(crossed, crossed_in, x_s, x_r, i).wait_recv()
        value = (
            buf[i, core, x].astype(f32)
            + buf_in[i, x].astype(f32)
            + crossed_in[i].astype(f32)
        ).astype(bf16)
        own_sum[i] = value
        if i > 0:
            to_owner(own_sum, dst, z_s, z_r, i).start()

    loads[0].wait()
    psum, esum = proj.at[0], back.at[0]
    pland, eland = proj.at[1], back.at[1]
    for i in range(n_ctx + 2):
        if i < n_ctx:
            s = source(i)
            value = None
            for p in range(PIECES):
                if i > 0:
                    att_copy(s, p, True).wait_recv()
                    chain_each(i, s, lambda right, s=s, p=p: att_copy(s, p, right).start())
                term = jnp.dot(
                    att[s, p],
                    wo[p * piece_width : (p + 1) * piece_width, :],
                    preferred_element_type=f32,
                )
                value = term if value is None else value + term
            store_chunk(part, i, slice(None), value)
            swap_core(part, part_in, pa_s, pa_r, i).start()
        if 1 <= i <= n_ctx:
            after_core(i - 1, part, part_in, cross, pa_s, pa_r, cross_in, px_s, px_r)
        if i >= 2:
            after_x(
                i - 2, part, part_in, cross_in, cross, px_s, px_r, pland, psum, pz_s, pz_r
            )

    def landed(dst, own_sum, send, recv, s):
        return to_ctx(own_sum.at[0], dst.at[s], send.at[0], recv.at[s], (z + 1) % n_ctx)

    pland[z] = psum[0]
    for i in range(1, n_ctx):
        landed(pland, psum, pz_s, pz_r, source(i)).wait_recv()
    squares = jnp.zeros((own, 1), f32)
    for s in range(n_ctx):
        columns = slice(s * block, (s + 1) * block)
        value = (pland[s].astype(f32) + res_ref[:, columns].astype(f32)).astype(bf16)
        mixed_ref[:, columns] = value
        value = value.astype(f32)
        squares = squares + jnp.sum(value * value, axis=-1, keepdims=True)
    factor = lax.rsqrt(squares / model + 1e-06)
    tok[z, h, :, :model] = (mixed_ref[...].astype(f32) * factor * gain_ref[...]).astype(bf16)

    def tok_z(s, go_right):
        return chain(tok.at[s, h], tz_s.at[s], tz_r.at[s], s, go_right)

    def tok_x(s):
        return to_head(tok.at[s, h], tok.at[s, h], tx_s.at[s], tx_r.at[s], x_peer)

    def tok_c(s, which):
        b = h if which == 0 else x_peer
        return to_head(tok.at[s, b], tok.at[s, b], tc_s.at[s, which], tc_r.at[s, which], core_peer)

    for load in loads[1:]:
        load.wait()
    tile = 256
    expert = z * lax.axis_size("head") + h

    def experts(i, s):
        tokens = tok[s, :, :, :model].reshape(4 * own, model)
        table = tok[s, :, :, model:].reshape(4 * own, LANES).astype(f32)
        at = lax.broadcasted_iota(jnp.int32, table.shape, 1)
        weight = jnp.sum(jnp.where(at % half == expert, table, 0.0), axis=-1, keepdims=True)
        acts = []
        for t in range(hidden // tile):
            columns = slice(t * tile, (t + 1) * tile)
            gate_act = jnp.dot(tokens, wg[:, columns], preferred_element_type=f32)
            up_act = jnp.dot(tokens, wu[:, columns], preferred_element_type=f32)
            acts.append((gate_act * (up_act / (1.0 + jnp.exp(-gate_act)))).astype(bf16))
        hid = jnp.concatenate(acts, axis=1)

        @pl.loop(0, model // tile)
        def _(t):
            columns = pl.ds(pl.multiple_of(t * tile, tile), tile)
            value = jnp.dot(hid, wd[:, columns], preferred_element_type=f32)
            store_chunk(epart, i, columns, value.astype(bf16).astype(f32) * weight)

    for i in range(n_ctx + 3):
        if i < n_ctx:
            s = source(i)
            if i > 0:
                tok_z(s, True).wait_recv()
            chain_each(i, s, lambda right, s=s: tok_z(s, right).start())
            tok_x(s).start()
            tok_c(s, 0).start()
        if 1 <= i <= n_ctx:
            s = source(i - 1)
            tok_x(s).wait_recv()
            tok_c(s, 1).start()
            tok_c(s, 0).wait_recv()
            tok_c(s, 1).wait_recv()
            experts(i - 1, s)
            swap_core(epart, epart_in, ea_s, ea_r, i - 1).start()
        if 2 <= i <= n_ctx + 1:
            after_core(i - 2, epart, epart_in, ecross, ea_s, ea_r, ecross_in, ex_s, ex_r)
        if i >= 3:
            after_x(
                i - 3, epart, epart_in, ecross_in, ecross, ex_s, ex_r, eland, esum, ez_s, ez_r
            )

    total = esum[0].astype(f32)
    for i in range(1, n_ctx):
        s = source(i)
        landed(eland, esum, ez_s, ez_r, s).wait_recv()
        total = total + eland[s].astype(f32)
    out_ref[...] = total.astype(bf16)

    for s in range(n_ctx):

        @pl.when((s <= z) & (z < last))
        def _():
            kv_copy(s).wait_send()

    for i in range(n_ctx):
        s = source(i)
        for p in range(PIECES):
            chain_each(i, s, lambda right, s=s, p=p: att_copy(s, p, right).wait_send())
        chain_each(i, s, lambda right, s=s: tok_z(s, right).wait_send())
        tok_x(s).wait_send()
        tok_c(s, 0).wait_send()
        tok_c(s, 1).wait_send()
        swap_core(part, part_in, pa_s, pa_r, i).wait_send()
        swap_core(epart, epart_in, ea_s, ea_r, i).wait_send()
        swap_x(cross, cross_in, px_s, px_r, i).wait_send()
        swap_x(ecross, ecross_in, ex_s, ex_r, i).wait_send()
        if i > 0:
            to_owner(psum, pland, pz_s, pz_r, i).wait_send()
            to_owner(esum, eland, ez_s, ez_r, i).wait_send()


def fused(query, keys, values, residual, o_weight, gain, routes, gates, w_gate, w_up, w_down):
    n = lax.axis_size("ctx")
    rows, width = query.shape
    own, model = residual.shape
    hidden = w_gate.shape[2]
    block = o_weight.shape[1]
    bf16 = jnp.bfloat16
    vmem = pl.BlockSpec(memory_space=pltpu.VMEM)
    hbm = pl.BlockSpec(memory_space=pl.ANY)
    dma = pltpu.SemaphoreType.DMA

    def sums(columns):
        return [
            pltpu.VMEM((n, 2, 2, own, columns), bf16),
            pltpu.VMEM((n, 2, own, columns), bf16),
            pltpu.VMEM((n, own, columns), bf16),
            pltpu.VMEM((n, own, columns), bf16),
            pltpu.VMEM((2, n, own, columns), bf16),
        ]

    flops = 2 * rows * (width * model // 1 + 2 * n * rows * width) + 24 * n * rows * model * hidden // 4
    return pl.pallas_call(
        lambda *refs: layer_kernel(n, *refs),
        out_shape=(
            jax.ShapeDtypeStruct(residual.shape, bf16),
            jax.ShapeDtypeStruct(residual.shape, bf16),
        ),
        in_specs=[vmem, vmem, vmem, vmem, hbm, vmem, vmem, vmem, hbm, hbm, hbm],
        out_specs=(vmem, vmem),
        scratch_shapes=[
            pltpu.VMEM(o_weight.shape, bf16),
            pltpu.VMEM(w_gate.shape[1:], bf16),
            pltpu.VMEM(w_up.shape[1:], bf16),
            pltpu.VMEM(w_down.shape[1:], bf16),
            pltpu.VMEM((n, 2, rows, HEAD_DIMENSION), bf16),
            pltpu.VMEM((n, PIECES, rows, width // PIECES), bf16),
            *sums(block),
            pltpu.VMEM((n, 4, own, model + LANES), bf16),
            *sums(model),
            dma((4,)),
            dma((n,)), dma((n,)),
            dma((n, PIECES, 2)), dma((n, PIECES)),
            dma((n,)), dma((n,)), dma((n,)), dma((n,)), dma((n,)), dma((n,)),
            dma((n, 2)), dma((n,)), dma((n,)), dma((n,)), dma((n, 2)), dma((n, 2)),
            dma((n,)), dma((n,)), dma((n,)), dma((n,)), dma((n,)), dma((n,)),
        ],
        compiler_params=pltpu.CompilerParams(
            collective_id=0, has_side_effects=True, vmem_limit_bytes=48 * 1024 * 1024
        ),
        cost_estimate=pl.CostEstimate(
            flops=flops, bytes_accessed=6 * model * hidden + 2 * width * block, transcendentals=0
        ),
        name="layer",
    )(
        query, keys, values, residual, o_weight, gain.reshape(1, -1), routes, gates,
        w_gate, w_up, w_down,
    )


def every_token_fits(mesh, *args):
    devices = mesh.shape["ctx"] * mesh.shape["head"]
    own = args[3].shape[0] // (devices * mesh.shape["group"])
    top = args[6].shape[1]
    capacity = min(own, max(2, 2 * own * top // devices))
    return (
        capacity == own
        and mesh.shape["head"] == 4
        and mesh.shape["ctx"] <= 8
        and args[8].shape[0] == devices
        and devices <= LANES // 2
        and own % 16 == 0
        and args[1].shape[1] == 4 * HEAD_DIMENSION
    )


def solution(mesh):
    def run(*args):
        inner = fused if every_token_fits(mesh, *args) else body
        return split(mesh, inner)(*args)

    return run


def split(mesh, inner):
    return jax.shard_map(
        inner,
        mesh=mesh,
        in_specs=(
            P(("group", "ctx"), "head"),
            P(("group", "ctx"), "head"),
            P(("group", "ctx"), "head"),
            P(("group", "ctx", "head"), None),
            P("head", "ctx"),
            P(),
            P(("group", "ctx", "head"), None),
            P(("group", "ctx", "head"), None),
            P(("ctx", "head"), None, None),
            P(("ctx", "head"), None, None),
            P(("ctx", "head"), None, None),
        ),
        out_specs=(P(("group", "ctx", "head"), None), P(("group", "ctx", "head"), None)),
        check_vma=False,
    )
```

```python
import jax
import jax.numpy as jnp
from jax import lax
from jax.experimental import pallas as pl
from jax.experimental.pallas import tpu as pltpu
from jax.sharding import PartitionSpec as P

HEAD_DIMENSION = 128


def expert_apply(arrived, gate_proj, up_proj, down_proj):
    shape_in = arrived.shape
    flat_rows = arrived.reshape(-1, shape_in[-1])
    gate_act = jnp.dot(flat_rows, gate_proj, preferred_element_type=jnp.float32)
    up_act = jnp.dot(flat_rows, up_proj, preferred_element_type=jnp.float32)
    hidden = (jax.nn.silu(gate_act) * up_act).astype(jnp.bfloat16)
    output = jnp.dot(hidden, down_proj, preferred_element_type=jnp.float32).astype(jnp.bfloat16)
    return output.reshape(shape_in)


def body(query, keys, values, residual, o_weight, gain, routes, gates, w_gate, w_up, w_down):
    head_size = HEAD_DIMENSION
    query_rows = query.shape[0]
    kv_heads = keys.shape[1] // head_size
    q_heads = query.shape[1] // head_size
    head_replicas = q_heads // kv_heads
    scale = head_size ** (-0.5)
    queries = query.reshape(query_rows, kv_heads, head_replicas, head_size)
    first_pos = lax.axis_index("ctx") * query_rows
    query_pos = first_pos + jnp.arange(query_rows, dtype=jnp.int32)
    last_pos = first_pos + query_rows - 1

    def accumulate(carry, pieces):
        run_max, run_sum, run_acc = carry
        key_piece, value_piece = pieces
        width = key_piece.shape[0]
        key_pos = jnp.arange(width, dtype=jnp.int32)
        visible = key_pos[None, :] <= query_pos[:, None]
        scores = (
            jnp.einsum(
                "veqi,zei->eqvz",
                queries,
                key_piece.reshape(width, kv_heads, head_size),
                preferred_element_type=jnp.float32,
            )
            * scale
        )
        scores = jnp.where(visible, scores, -1e30)
        new_max = jnp.maximum(run_max, jnp.max(scores, axis=-1))
        weights = jnp.where(visible, jnp.exp(scores - new_max[..., None]), 0.0)
        new_sum = jnp.sum(weights, axis=-1)
        update = jnp.einsum(
            "pexa,apo->pexo",
            weights.astype(jnp.bfloat16),
            value_piece.reshape(width, kv_heads, head_size),
            preferred_element_type=jnp.float32,
        )
        return (new_max, new_sum, update)

    start_state = (
        jnp.full((kv_heads, head_replicas, query_rows), -1e30, jnp.float32),
        jnp.zeros((kv_heads, head_replicas, query_rows), jnp.float32),
        jnp.zeros((kv_heads, head_replicas, query_rows, head_size), jnp.float32),
    )
    pieces = (
        lax.all_gather(keys, "ctx", axis=0, tiled=True),
        lax.all_gather(values, "ctx", axis=0, tiled=True),
    )
    run_max, run_sum, run_acc = lax.cond(
        jnp.int32(0) > last_pos, lambda: start_state, lambda: accumulate(start_state, pieces)
    )
    attended = (
        (run_acc / run_sum[..., None])
        .transpose(2, 0, 1, 3)
        .reshape(query_rows, q_heads * head_size)
        .astype(jnp.bfloat16)
    )
    head_terms = jnp.dot(
        attended,
        lax.all_gather(o_weight, "ctx", axis=1, tiled=True),
        preferred_element_type=jnp.float32,
    )
    summed = lax.psum_scatter(
        head_terms.astype(jnp.bfloat16), "head", scatter_dimension=0, tiled=True
    ).astype(jnp.float32)
    mixed = (summed + residual.astype(jnp.float32)).astype(jnp.bfloat16)
    mixed_f = mixed.astype(jnp.float32)
    normed = (
        mixed_f * lax.rsqrt(jnp.mean(mixed_f * mixed_f, axis=-1, keepdims=True) + 1e-06) * gain
    ).astype(jnp.bfloat16)
    own_rows = residual.shape[0]
    model_dim = residual.shape[1]
    top_count = routes.shape[1]
    ctx_count = lax.axis_size("ctx")
    head_count = lax.axis_size("head")
    devices = ctx_count * head_count
    capacity = min(own_rows, max(2, 2 * own_rows * top_count // devices))
    expert_ids = routes.reshape(-1)
    onehot = (expert_ids[:, None] == jnp.arange(devices, dtype=jnp.int32)[None, :]).astype(
        jnp.int32
    )
    slots = jnp.sum((jnp.cumsum(onehot, axis=0) - 1) * onehot, axis=1)
    target = expert_ids * capacity + slots
    outgoing = (
        jnp.zeros((devices * capacity, model_dim), jnp.bfloat16)
        .at[target]
        .set(jnp.repeat(normed, top_count, axis=0))
    )
    outgoing = outgoing.reshape(devices, capacity, model_dim)
    gate_proj = w_gate[0]
    up_proj = w_up[0]
    down_proj = w_down[0]
    computed = expert_apply(
        lax.all_to_all(outgoing, ("ctx", "head"), split_axis=0, concat_axis=0, tiled=True),
        gate_proj,
        up_proj,
        down_proj,
    )
    returned = lax.all_to_all(computed, ("ctx", "head"), split_axis=0, concat_axis=0, tiled=True)
    selected_entries = returned.reshape(devices * capacity, model_dim)[target]
    selected_entries = selected_entries.astype(jnp.float32).reshape(own_rows, top_count, model_dim)
    weight_norm = gates / jnp.sum(gates, axis=-1, keepdims=True)
    expert_mix = jnp.sum(selected_entries * weight_norm[..., None], axis=1).astype(jnp.bfloat16)
    return (mixed, expert_mix)


LANES = 128
PIECES = 2
CUT = 2
MESH = pl.DeviceIdType.MESH


def layer_kernel(
    n_ctx,
    q_hbm, k_hbm, v_hbm, res_hbm, wo_hbm, gain_hbm, routes_hbm, gates_hbm, wg_hbm, wu_hbm, wd_hbm,
    mixed_ref, out_ref,
    q_ref, res_ref, gain_ref, routes_ref, gates_ref, wo, wg, wu, wd,
    kv, att, part, part_in, cross, cross_in, proj,
    tok, epart, epart_in, ecross, ecross_in, back,
    local_sem,
    kv_s, kv_r, att_s, att_r, pa_s, pa_r, px_s, px_r, pz_s, pz_r,
    tz_s, tz_r, tx_s, tx_r, tc_s, tc_r, ea_s, ea_r, ex_s, ex_r, ez_s, ez_r,
):
    f32, bf16 = jnp.float32, jnp.bfloat16
    z = lax.axis_index("ctx")
    h = lax.axis_index("head")
    x, core = h // 2, h % 2
    core_peer = x * 2 + (1 - core)
    x_peer = (1 - x) * 2 + core
    rows, own, model = q_ref.shape[0], res_ref.shape[0], res_ref.shape[1]
    size = HEAD_DIMENSION
    q_heads = q_ref.shape[1] // size
    piece_heads = q_heads // PIECES
    piece_width = piece_heads * size
    block = model // n_ctx
    hidden = wg.shape[1]

    loads = [
        pltpu.make_async_copy(src, dst, local_sem.at[i])
        for i, (src, dst) in enumerate(
            (
                (k_hbm, kv.at[z, 0]),
                (v_hbm, kv.at[z, 1]),
                (routes_hbm, routes_ref),
                (gates_hbm, gates_ref),
                (q_hbm, q_ref),
                (wo_hbm, wo),
                (res_hbm, res_ref),
                (gain_hbm, gain_ref),
                (wg_hbm.at[0], wg),
                (wu_hbm.at[0], wu),
                (wd_hbm.at[0], wd),
            )
        )
    ]
    for load in loads:
        load.start()

    barrier = pltpu.get_barrier_semaphore()
    for peer in (core_peer, x_peer):
        pl.semaphore_signal(barrier, inc=1, device_id={"head": peer}, device_id_type=MESH)
    for step in range(1, n_ctx):
        pl.semaphore_signal(
            barrier, inc=1, device_id={"ctx": (z + step) % n_ctx}, device_id_type=MESH
        )

    for other in range(1, n_ctx):

        @pl.when(z < other)
        def _():
            kv[other] = jnp.zeros(kv.shape[1:], bf16)

    loads[2].wait()
    loads[3].wait()
    gate_values = gates_ref[...].T
    gate_norm = gate_values / jnp.sum(gate_values, axis=-1, keepdims=True)
    route_values = routes_ref[...].T
    lane = lax.broadcasted_iota(jnp.int32, (own, LANES), 1)
    half = LANES // 2
    table = jnp.zeros((own, LANES), f32)
    for k in range(route_values.shape[1]):
        table = table + jnp.where(
            lane % half == route_values[:, k : k + 1], gate_norm[:, k : k + 1], 0.0
        )
    high = table.astype(bf16).astype(f32)
    tok[z, h, :, model:] = jnp.where(lane < half, high, table - high).astype(bf16)

    pl.semaphore_wait(barrier, n_ctx + 1)

    def to_ctx(src, dst, send, recv, target):
        return pltpu.make_async_remote_copy(
            src_ref=src, dst_ref=dst, send_sem=send, recv_sem=recv,
            device_id={"ctx": target}, device_id_type=MESH,
        )

    def to_head(src, dst, send, recv, target):
        return pltpu.make_async_remote_copy(
            src_ref=src, dst_ref=dst, send_sem=send, recv_sem=recv,
            device_id={"head": target}, device_id_type=MESH,
        )

    last = n_ctx - 1
    short = jnp.minimum(z, last - z)
    toward = jnp.where(z * 2 < last, -1, 1)

    def source(i):
        if i == 0:
            return z
        near = toward * ((i + 1) // 2) if i % 2 else -toward * (i // 2)
        return z + jnp.where(i <= 2 * short, near, -toward * (i - short))

    def kv_copy(s, step):
        return to_ctx(
            kv.at[s], kv.at[s], kv_s.at[step], kv_r.at[s], jnp.minimum(z + step, last)
        )

    loads[0].wait()
    loads[1].wait()
    for step in range(1, n_ctx):

        @pl.when(z + step <= last)
        def _():
            kv_copy(z, step).start()

    loads[4].wait()
    for step in range(1, n_ctx):

        @pl.when(z >= step)
        def _():
            kv_copy(z - step, step).wait_recv()

    def chain(buf_at, send, recv, s, go_right):
        way = 1 if go_right else 0
        target = jnp.clip(z + (1 if go_right else -1), 0, last)
        return to_ctx(buf_at, buf_at, send.at[way], recv, target)

    def chain_each(i, s, run):
        @pl.when((s <= z) & (z < last))
        def _():
            run(True)

        @pl.when((s >= z) & (z > 0))
        def _():
            run(False)

    def att_copy(s, p, go_right):
        return chain(att.at[s, p], att_s.at[s, p], att_r.at[s, p], s, go_right)

    keys_all = kv[:, 0].reshape(n_ctx * rows, size)
    values_all = kv[:, 1].reshape(n_ctx * rows, size)
    row_at = lax.broadcasted_iota(jnp.int32, (rows, n_ctx * rows), 0)
    col_at = lax.broadcasted_iota(jnp.int32, (rows, n_ctx * rows), 1)
    visible = col_at <= row_at + z * rows
    scale = size ** (-0.5)
    for p in range(PIECES):
        for j in range(piece_heads):
            head = p * piece_heads + j
            scores = lax.dot_general(
                q_ref[:, head * size : (head + 1) * size],
                keys_all,
                (((1,), (1,)), ((), ())),
                preferred_element_type=f32,
            )
            scores = jnp.where(visible, scores * scale, -1e30)
            top = jnp.max(scores, axis=-1, keepdims=True)
            weights = jnp.where(visible, jnp.exp(scores - top), 0.0)
            total = jnp.sum(weights, axis=-1, keepdims=True)
            summed = jnp.dot(weights.astype(bf16), values_all, preferred_element_type=f32)
            att[z, p, :, j * size : (j + 1) * size] = (summed / total).astype(bf16)
        chain_each(0, z, lambda right, p=p: att_copy(z, p, right).start())

    def swap_core(buf, buf_in, send, recv, i):
        return to_head(buf.at[i, 1 - core], buf_in.at[i], send.at[i], recv.at[i], core_peer)

    def swap_x(buf, buf_in, send, recv, i):
        return to_head(buf.at[i], buf_in.at[i], send.at[i], recv.at[i], x_peer)

    def to_owner(buf, dst, send, recv, i, cut):
        slot = z * cut + i % cut
        return to_ctx(buf.at[i], dst.at[slot], send.at[i], recv.at[slot], source(i // cut))

    def store_chunk(buf, i, columns, value):
        parts = value.astype(bf16).reshape(2, 2, own, value.shape[-1])
        for cc in range(2):
            for xx in range(2):
                buf[i, cc, xx, :, columns] = parts[xx, cc]

    def after_core(i, buf, buf_in, crossed, a_s, a_r, crossed_in, x_s, x_r):
        swap_core(buf, buf_in, a_s, a_r, i).wait_recv()
        crossed[i] = (
            buf[i, core, 1 - x].astype(f32) + buf_in[i, 1 - x].astype(f32)
        ).astype(bf16)
        swap_x(crossed, crossed_in, x_s, x_r, i).start()

    def after_x(i, buf, buf_in, crossed_in, crossed, x_s, x_r, dst, own_sum, z_s, z_r, cut):
        swap_x(crossed, crossed_in, x_s, x_r, i).wait_recv()
        value = (
            buf[i, core, x].astype(f32)
            + buf_in[i, x].astype(f32)
            + crossed_in[i].astype(f32)
        ).astype(bf16)
        own_sum[i] = value
        if i >= cut:
            to_owner(own_sum, dst, z_s, z_r, i, cut).start()

    loads[5].wait()
    psum, esum = proj.at[0], back.at[0]
    pland, eland = proj.at[1], back.at[1]
    for i in range(n_ctx + 2):
        if i < n_ctx:
            s = source(i)
            value = None
            for p in range(PIECES):
                if i > 0:
                    att_copy(s, p, True).wait_recv()
                    chain_each(i, s, lambda right, s=s, p=p: att_copy(s, p, right).start())
                term = jnp.dot(
                    att[s, p],
                    wo[p * piece_width : (p + 1) * piece_width, :],
                    preferred_element_type=f32,
                )
                value = term if value is None else value + term
            store_chunk(part, i, slice(None), value)
            swap_core(part, part_in, pa_s, pa_r, i).start()
        if 1 <= i <= n_ctx:
            after_core(i - 1, part, part_in, cross, pa_s, pa_r, cross_in, px_s, px_r)
        if i >= 2:
            after_x(
                i - 2, part, part_in, cross_in, cross, px_s, px_r, pland, psum, pz_s, pz_r, 1
            )

    def landed(dst, own_sum, send, recv, s):
        return to_ctx(own_sum.at[0], dst.at[s], send.at[0], recv.at[s], (z + 1) % n_ctx)

    loads[6].wait()
    loads[7].wait()
    pland[z] = psum[0]
    for i in range(1, n_ctx):
        landed(pland, psum, pz_s, pz_r, source(i)).wait_recv()
    squares = jnp.zeros((own, 1), f32)
    for s in range(n_ctx):
        columns = slice(s * block, (s + 1) * block)
        value = (pland[s].astype(f32) + res_ref[:, columns].astype(f32)).astype(bf16)
        mixed_ref[:, columns] = value
        value = value.astype(f32)
        squares = squares + jnp.sum(value * value, axis=-1, keepdims=True)
    factor = lax.rsqrt(squares / model + 1e-06)
    tok[z, h, :, :model] = (mixed_ref[...].astype(f32) * factor * gain_ref[...]).astype(bf16)

    def tok_z(s, go_right):
        return chain(tok.at[s, h], tz_s.at[s], tz_r.at[s], s, go_right)

    def tok_x(s):
        return to_head(tok.at[s, h], tok.at[s, h], tx_s.at[s], tx_r.at[s], x_peer)

    def tok_c(s, which):
        b = h if which == 0 else x_peer
        return to_head(tok.at[s, b], tok.at[s, b], tc_s.at[s, which], tc_r.at[s, which], core_peer)

    for load in loads[8:]:
        load.wait()
    tile = 256
    expert = z * lax.axis_size("head") + h

    def hidden_of(s):
        tokens = tok[s, :, :, :model].reshape(4 * own, model)
        table = tok[s, :, :, model:].reshape(4 * own, LANES).astype(f32)
        at = lax.broadcasted_iota(jnp.int32, table.shape, 1)
        weight = jnp.sum(jnp.where(at % half == expert, table, 0.0), axis=-1, keepdims=True)
        acts = []
        for t in range(hidden // tile):
            columns = slice(t * tile, (t + 1) * tile)
            gate_act = jnp.dot(tokens, wg[:, columns], preferred_element_type=f32)
            up_act = jnp.dot(tokens, wu[:, columns], preferred_element_type=f32)
            acts.append((gate_act * (up_act / (1.0 + jnp.exp(-gate_act)))).astype(bf16))
        return jnp.concatenate(acts, axis=1), weight

    width = model // CUT

    def output_of(i, hid, weight):
        first = (i % CUT) * width

        @pl.loop(0, width // tile)
        def _(t):
            columns = pl.ds(pl.multiple_of(t * tile, tile), tile)
            source_columns = pl.ds(pl.multiple_of(first + t * tile, tile), tile)
            value = jnp.dot(hid, wd[:, source_columns], preferred_element_type=f32)
            store_chunk(epart, i, columns, value.astype(bf16).astype(f32) * weight)

        swap_core(epart, epart_in, ea_s, ea_r, i).start()

    def experts_core(i):
        after_core(i, epart, epart_in, ecross, ea_s, ea_r, ecross_in, ex_s, ex_r)

    def experts_x(i):
        after_x(
            i, epart, epart_in, ecross_in, ecross, ex_s, ex_r, eland, esum, ez_s, ez_r, CUT
        )

    for i in range(n_ctx + 2):
        if i < n_ctx:
            s = source(i)
            if i > 0:
                tok_z(s, True).wait_recv()
            chain_each(i, s, lambda right, s=s: tok_z(s, right).start())
            tok_x(s).start()
            tok_c(s, 0).start()
        if 1 <= i <= n_ctx:
            s = source(i - 1)
            tok_x(s).wait_recv()
            tok_c(s, 1).start()
            tok_c(s, 0).wait_recv()
            tok_c(s, 1).wait_recv()
            hid, weight = hidden_of(s)
        if i >= 2:
            for c in range(CUT):
                experts_core((i - 2) * CUT + c)
        for c in range(CUT):
            if 1 <= i <= n_ctx:
                output_of((i - 1) * CUT + c, hid, weight)
            if i >= 2:
                experts_x((i - 2) * CUT + c)

    for c in range(CUT):
        total = esum[c].astype(f32)
        for i in range(1, n_ctx):
            slot = source(i) * CUT + c
            landed(eland, esum, ez_s, ez_r, slot).wait_recv()
            total = total + eland[slot].astype(f32)
        out_ref[:, c * width : (c + 1) * width] = total.astype(bf16)

    for step in range(1, n_ctx):

        @pl.when(z + step <= last)
        def _():
            kv_copy(z, step).wait_send()

    for i in range(n_ctx):
        s = source(i)
        for p in range(PIECES):
            chain_each(i, s, lambda right, s=s, p=p: att_copy(s, p, right).wait_send())
        chain_each(i, s, lambda right, s=s: tok_z(s, right).wait_send())
        tok_x(s).wait_send()
        tok_c(s, 0).wait_send()
        tok_c(s, 1).wait_send()
        swap_core(part, part_in, pa_s, pa_r, i).wait_send()
        swap_x(cross, cross_in, px_s, px_r, i).wait_send()
        if i > 0:
            to_owner(psum, pland, pz_s, pz_r, i, 1).wait_send()
    for i in range(n_ctx * CUT):
        swap_core(epart, epart_in, ea_s, ea_r, i).wait_send()
        swap_x(ecross, ecross_in, ex_s, ex_r, i).wait_send()
        if i >= CUT:
            to_owner(esum, eland, ez_s, ez_r, i, CUT).wait_send()


def fused(query, keys, values, residual, o_weight, gain, routes, gates, w_gate, w_up, w_down):
    n = lax.axis_size("ctx")
    rows, width = query.shape
    own, model = residual.shape
    hidden = w_gate.shape[2]
    block = o_weight.shape[1]
    bf16 = jnp.bfloat16
    vmem = pl.BlockSpec(memory_space=pltpu.VMEM)
    hbm = pl.BlockSpec(memory_space=pltpu.HBM)
    dma = pltpu.SemaphoreType.DMA

    def sums(slots, columns):
        return [
            pltpu.VMEM((slots, 2, 2, own, columns), bf16),
            pltpu.VMEM((slots, 2, own, columns), bf16),
            pltpu.VMEM((slots, own, columns), bf16),
            pltpu.VMEM((slots, own, columns), bf16),
            pltpu.VMEM((2, slots, own, columns), bf16),
        ]

    flops = 2 * rows * (width * model // 1 + 2 * n * rows * width) + 24 * n * rows * model * hidden // 4
    return pl.pallas_call(
        lambda *refs: layer_kernel(n, *refs),
        out_shape=(
            jax.ShapeDtypeStruct(residual.shape, bf16),
            jax.ShapeDtypeStruct(residual.shape, bf16),
        ),
        in_specs=[hbm] * 11,
        out_specs=(vmem, vmem),
        scratch_shapes=[
            pltpu.VMEM(query.shape, bf16),
            pltpu.VMEM(residual.shape, bf16),
            pltpu.VMEM((1, model), jnp.float32),
            pltpu.VMEM(routes.shape[::-1], jnp.int32),
            pltpu.VMEM(gates.shape[::-1], jnp.float32),
            pltpu.VMEM(o_weight.shape, bf16),
            pltpu.VMEM(w_gate.shape[1:], bf16),
            pltpu.VMEM(w_up.shape[1:], bf16),
            pltpu.VMEM(w_down.shape[1:], bf16),
            pltpu.VMEM((n, 2, rows, HEAD_DIMENSION), bf16),
            pltpu.VMEM((n, PIECES, rows, width // PIECES), bf16),
            *sums(n, block),
            pltpu.VMEM((n, 4, own, model + LANES), bf16),
            *sums(n * CUT, model // CUT),
            dma((11,)),
            dma((n,)), dma((n,)),
            dma((n, PIECES, 2)), dma((n, PIECES)),
            dma((n,)), dma((n,)), dma((n,)), dma((n,)), dma((n,)), dma((n,)),
            dma((n, 2)), dma((n,)), dma((n,)), dma((n,)), dma((n, 2)), dma((n, 2)),
            *[dma((n * CUT,))] * 6,
        ],
        compiler_params=pltpu.CompilerParams(
            collective_id=0, has_side_effects=True, vmem_limit_bytes=56 * 1024 * 1024
        ),
        cost_estimate=pl.CostEstimate(
            flops=flops, bytes_accessed=6 * model * hidden + 2 * width * block, transcendentals=0
        ),
        name="layer",
    )(
        query, keys, values, residual, o_weight, gain.reshape(1, -1), routes.T, gates.T,
        w_gate, w_up, w_down,
    )


def every_token_fits(mesh, *args):
    devices = mesh.shape["ctx"] * mesh.shape["head"]
    own = args[3].shape[0] // (devices * mesh.shape["group"])
    top = args[6].shape[1]
    capacity = min(own, max(2, 2 * own * top // devices))
    return (
        capacity == own
        and mesh.shape["head"] == 4
        and mesh.shape["ctx"] <= 8
        and args[8].shape[0] == devices
        and devices <= LANES // 2
        and own % 16 == 0
        and args[1].shape[1] == 4 * HEAD_DIMENSION
    )


def solution(mesh):
    def run(*args):
        inner = fused if every_token_fits(mesh, *args) else body
        return split(mesh, inner)(*args)

    return run


def split(mesh, inner):
    return jax.shard_map(
        inner,
        mesh=mesh,
        in_specs=(
            P(("group", "ctx"), "head"),
            P(("group", "ctx"), "head"),
            P(("group", "ctx"), "head"),
            P(("group", "ctx", "head"), None),
            P("head", "ctx"),
            P(),
            P(("group", "ctx", "head"), None),
            P(("group", "ctx", "head"), None),
            P(("ctx", "head"), None, None),
            P(("ctx", "head"), None, None),
            P(("ctx", "head"), None, None),
        ),
        out_specs=(P(("group", "ctx", "head"), None), P(("group", "ctx", "head"), None)),
        check_vma=False,
    )
```

```python
import jax
import jax.numpy as jnp
from jax import lax
from jax.experimental import pallas as pl
from jax.experimental.pallas import tpu as pltpu
from jax.sharding import PartitionSpec as P

HEAD_DIMENSION = 128


def expert_apply(arrived, gate_proj, up_proj, down_proj):
    shape_in = arrived.shape
    flat_rows = arrived.reshape(-1, shape_in[-1])
    gate_act = jnp.dot(flat_rows, gate_proj, preferred_element_type=jnp.float32)
    up_act = jnp.dot(flat_rows, up_proj, preferred_element_type=jnp.float32)
    hidden = (jax.nn.silu(gate_act) * up_act).astype(jnp.bfloat16)
    output = jnp.dot(hidden, down_proj, preferred_element_type=jnp.float32).astype(jnp.bfloat16)
    return output.reshape(shape_in)


def body(query, keys, values, residual, o_weight, gain, routes, gates, w_gate, w_up, w_down):
    head_size = HEAD_DIMENSION
    query_rows = query.shape[0]
    kv_heads = keys.shape[1] // head_size
    q_heads = query.shape[1] // head_size
    head_replicas = q_heads // kv_heads
    scale = head_size ** (-0.5)
    queries = query.reshape(query_rows, kv_heads, head_replicas, head_size)
    first_pos = lax.axis_index("ctx") * query_rows
    query_pos = first_pos + jnp.arange(query_rows, dtype=jnp.int32)
    last_pos = first_pos + query_rows - 1

    def accumulate(carry, pieces):
        run_max, run_sum, run_acc = carry
        key_piece, value_piece = pieces
        width = key_piece.shape[0]
        key_pos = jnp.arange(width, dtype=jnp.int32)
        visible = key_pos[None, :] <= query_pos[:, None]
        scores = (
            jnp.einsum(
                "veqi,zei->eqvz",
                queries,
                key_piece.reshape(width, kv_heads, head_size),
                preferred_element_type=jnp.float32,
            )
            * scale
        )
        scores = jnp.where(visible, scores, -1e30)
        new_max = jnp.maximum(run_max, jnp.max(scores, axis=-1))
        weights = jnp.where(visible, jnp.exp(scores - new_max[..., None]), 0.0)
        new_sum = jnp.sum(weights, axis=-1)
        update = jnp.einsum(
            "pexa,apo->pexo",
            weights.astype(jnp.bfloat16),
            value_piece.reshape(width, kv_heads, head_size),
            preferred_element_type=jnp.float32,
        )
        return (new_max, new_sum, update)

    start_state = (
        jnp.full((kv_heads, head_replicas, query_rows), -1e30, jnp.float32),
        jnp.zeros((kv_heads, head_replicas, query_rows), jnp.float32),
        jnp.zeros((kv_heads, head_replicas, query_rows, head_size), jnp.float32),
    )
    pieces = (
        lax.all_gather(keys, "ctx", axis=0, tiled=True),
        lax.all_gather(values, "ctx", axis=0, tiled=True),
    )
    run_max, run_sum, run_acc = lax.cond(
        jnp.int32(0) > last_pos, lambda: start_state, lambda: accumulate(start_state, pieces)
    )
    attended = (
        (run_acc / run_sum[..., None])
        .transpose(2, 0, 1, 3)
        .reshape(query_rows, q_heads * head_size)
        .astype(jnp.bfloat16)
    )
    head_terms = jnp.dot(
        attended,
        lax.all_gather(o_weight, "ctx", axis=1, tiled=True),
        preferred_element_type=jnp.float32,
    )
    summed = lax.psum_scatter(
        head_terms.astype(jnp.bfloat16), "head", scatter_dimension=0, tiled=True
    ).astype(jnp.float32)
    mixed = (summed + residual.astype(jnp.float32)).astype(jnp.bfloat16)
    mixed_f = mixed.astype(jnp.float32)
    normed = (
        mixed_f * lax.rsqrt(jnp.mean(mixed_f * mixed_f, axis=-1, keepdims=True) + 1e-06) * gain
    ).astype(jnp.bfloat16)
    own_rows = residual.shape[0]
    model_dim = residual.shape[1]
    top_count = routes.shape[1]
    ctx_count = lax.axis_size("ctx")
    head_count = lax.axis_size("head")
    devices = ctx_count * head_count
    capacity = min(own_rows, max(2, 2 * own_rows * top_count // devices))
    expert_ids = routes.reshape(-1)
    onehot = (expert_ids[:, None] == jnp.arange(devices, dtype=jnp.int32)[None, :]).astype(
        jnp.int32
    )
    slots = jnp.sum((jnp.cumsum(onehot, axis=0) - 1) * onehot, axis=1)
    target = expert_ids * capacity + slots
    outgoing = (
        jnp.zeros((devices * capacity, model_dim), jnp.bfloat16)
        .at[target]
        .set(jnp.repeat(normed, top_count, axis=0))
    )
    outgoing = outgoing.reshape(devices, capacity, model_dim)
    gate_proj = w_gate[0]
    up_proj = w_up[0]
    down_proj = w_down[0]
    computed = expert_apply(
        lax.all_to_all(outgoing, ("ctx", "head"), split_axis=0, concat_axis=0, tiled=True),
        gate_proj,
        up_proj,
        down_proj,
    )
    returned = lax.all_to_all(computed, ("ctx", "head"), split_axis=0, concat_axis=0, tiled=True)
    selected_entries = returned.reshape(devices * capacity, model_dim)[target]
    selected_entries = selected_entries.astype(jnp.float32).reshape(own_rows, top_count, model_dim)
    weight_norm = gates / jnp.sum(gates, axis=-1, keepdims=True)
    expert_mix = jnp.sum(selected_entries * weight_norm[..., None], axis=1).astype(jnp.bfloat16)
    return (mixed, expert_mix)


LANES = 128
PIECES = 2
CUT = 2
MESH = pl.DeviceIdType.MESH


def layer_kernel(
    n_ctx,
    q_hbm, k_hbm, v_hbm, res_hbm, wo_hbm, gain_hbm, routes_hbm, gates_hbm, wg_hbm, wu_hbm, wd_hbm,
    mixed_ref, out_ref,
    q_ref, res_ref, gain_ref, routes_ref, gates_ref, wo, wg, wu, wd,
    kv, att, part, part_in, proj,
    tok, epart, epart_in, ecross, ecross_in, back,
    local_sem,
    kv_s, kv_r, att_s, att_r, pa_s, pa_r, pz_s, pz_r,
    tz_s, tz_r, tx_s, tx_r, tc_s, tc_r, ea_s, ea_r, ex_s, ex_r, ez_s, ez_r,
):
    f32, bf16 = jnp.float32, jnp.bfloat16
    z = lax.axis_index("ctx")
    h = lax.axis_index("head")
    x, core = h // 2, h % 2
    core_peer = x * 2 + (1 - core)
    x_peer = (1 - x) * 2 + core
    rows, own, model = q_ref.shape[0], res_ref.shape[0], res_ref.shape[1]
    size = HEAD_DIMENSION
    q_heads = q_ref.shape[1] // size
    piece_heads = q_heads // PIECES
    piece_width = piece_heads * size
    block = model // n_ctx
    hidden = wg.shape[1]

    loads = [
        pltpu.make_async_copy(src, dst, local_sem.at[i])
        for i, (src, dst) in enumerate(
            (
                (k_hbm, kv.at[z, 0]),
                (v_hbm, kv.at[z, 1]),
                (routes_hbm, routes_ref),
                (gates_hbm, gates_ref),
                (q_hbm, q_ref),
                (wo_hbm, wo),
                (res_hbm, res_ref),
                (gain_hbm, gain_ref),
                (wg_hbm.at[0], wg),
                (wu_hbm.at[0], wu),
                (wd_hbm.at[0], wd),
            )
        )
    ]
    for load in loads:
        load.start()

    barrier = pltpu.get_barrier_semaphore()
    n_head = lax.axis_size("head")
    for step in range(1, n_head):
        pl.semaphore_signal(
            barrier, inc=1, device_id={"head": (h + step) % n_head}, device_id_type=MESH
        )
    for step in range(1, n_ctx):
        pl.semaphore_signal(
            barrier, inc=1, device_id={"ctx": (z + step) % n_ctx}, device_id_type=MESH
        )

    for other in range(1, n_ctx):

        @pl.when(z < other)
        def _():
            kv[other] = jnp.zeros(kv.shape[1:], bf16)

    loads[2].wait()
    loads[3].wait()
    gate_values = gates_ref[...].T
    gate_norm = gate_values / jnp.sum(gate_values, axis=-1, keepdims=True)
    route_values = routes_ref[...].T
    lane = lax.broadcasted_iota(jnp.int32, (own, LANES), 1)
    half = LANES // 2
    table = jnp.zeros((own, LANES), f32)
    for k in range(route_values.shape[1]):
        table = table + jnp.where(
            lane % half == route_values[:, k : k + 1], gate_norm[:, k : k + 1], 0.0
        )
    high = table.astype(bf16).astype(f32)
    tok[z, h, :, model:] = jnp.where(lane < half, high, table - high).astype(bf16)

    pl.semaphore_wait(barrier, n_ctx + n_head - 2)

    def to_ctx(src, dst, send, recv, target):
        return pltpu.make_async_remote_copy(
            src_ref=src, dst_ref=dst, send_sem=send, recv_sem=recv,
            device_id={"ctx": target}, device_id_type=MESH,
        )

    def to_head(src, dst, send, recv, target):
        return pltpu.make_async_remote_copy(
            src_ref=src, dst_ref=dst, send_sem=send, recv_sem=recv,
            device_id={"head": target}, device_id_type=MESH,
        )

    last = n_ctx - 1
    short = jnp.minimum(z, last - z)
    toward = jnp.where(z * 2 < last, -1, 1)

    def source(i):
        if i == 0:
            return z
        near = toward * ((i + 1) // 2) if i % 2 else -toward * (i // 2)
        return z + jnp.where(i <= 2 * short, near, -toward * (i - short))

    def kv_copy(s, step):
        return to_ctx(
            kv.at[s], kv.at[s], kv_s.at[step], kv_r.at[s], jnp.minimum(z + step, last)
        )

    loads[0].wait()
    loads[1].wait()
    for step in range(1, n_ctx):

        @pl.when(z + step <= last)
        def _():
            kv_copy(z, step).start()

    loads[4].wait()
    for step in range(1, n_ctx):

        @pl.when(z >= step)
        def _():
            kv_copy(z - step, step).wait_recv()

    def chain(buf_at, send, recv, s, go_right):
        way = 1 if go_right else 0
        target = jnp.clip(z + (1 if go_right else -1), 0, last)
        return to_ctx(buf_at, buf_at, send.at[way], recv, target)

    def chain_each(i, s, run):
        @pl.when((s <= z) & (z < last))
        def _():
            run(True)

        @pl.when((s >= z) & (z > 0))
        def _():
            run(False)

    def att_copy(s, p, go_right):
        return chain(att.at[s, p], att_s.at[s, p], att_r.at[s, p], s, go_right)

    keys_all = kv[:, 0].reshape(n_ctx * rows, size)
    values_all = kv[:, 1].reshape(n_ctx * rows, size)
    row_at = lax.broadcasted_iota(jnp.int32, (rows, n_ctx * rows), 0)
    col_at = lax.broadcasted_iota(jnp.int32, (rows, n_ctx * rows), 1)
    visible = col_at <= row_at + z * rows
    scale = size ** (-0.5)
    for p in range(PIECES):
        for j in range(piece_heads):
            head = p * piece_heads + j
            scores = lax.dot_general(
                q_ref[:, head * size : (head + 1) * size],
                keys_all,
                (((1,), (1,)), ((), ())),
                preferred_element_type=f32,
            )
            scores = jnp.where(visible, scores * scale, -1e30)
            top = jnp.max(scores, axis=-1, keepdims=True)
            weights = jnp.exp(scores - top)
            total = jnp.sum(weights, axis=-1, keepdims=True)
            summed = jnp.dot(weights.astype(bf16), values_all, preferred_element_type=f32)
            att[z, p, :, j * size : (j + 1) * size] = (summed / total).astype(bf16)
        chain_each(0, z, lambda right, p=p: att_copy(z, p, right).start())

    def swap_core(buf, buf_in, send, recv, i):
        return to_head(buf.at[i, 1 - core], buf_in.at[i], send.at[i], recv.at[i], core_peer)

    def swap_x(buf, buf_in, send, recv, i):
        return to_head(buf.at[i], buf_in.at[i], send.at[i], recv.at[i], x_peer)

    def to_owner(buf, dst, send, recv, i, cut):
        slot = z * cut + i % cut
        return to_ctx(buf.at[i], dst.at[slot], send.at[i], recv.at[slot], source(i // cut))

    def to_head_owner(i, step):
        peer = (h + step) % n_head
        return to_head(
            part.at[i, peer], part_in.at[i, step - 1],
            pa_s.at[i, step - 1], pa_r.at[i, step - 1], peer,
        )

    def store_chunk(buf, i, columns, value):
        parts = value.astype(bf16).reshape(2, 2, own, value.shape[-1])
        for cc in range(2):
            for xx in range(2):
                buf[i, cc, xx, :, columns] = parts[xx, cc]

    def after_core(i, buf, buf_in, crossed, a_s, a_r, crossed_in, x_s, x_r):
        swap_core(buf, buf_in, a_s, a_r, i).wait_recv()
        crossed[i] = (
            buf[i, core, 1 - x].astype(f32) + buf_in[i, 1 - x].astype(f32)
        ).astype(bf16)
        swap_x(crossed, crossed_in, x_s, x_r, i).start()

    def after_x(i, buf, buf_in, crossed_in, crossed, x_s, x_r, dst, own_sum, z_s, z_r, cut):
        swap_x(crossed, crossed_in, x_s, x_r, i).wait_recv()
        value = (
            buf[i, core, x].astype(f32)
            + buf_in[i, x].astype(f32)
            + crossed_in[i].astype(f32)
        ).astype(bf16)
        own_sum[i] = value
        if i >= cut:
            to_owner(own_sum, dst, z_s, z_r, i, cut).start()

    loads[5].wait()
    psum, esum = proj.at[0], back.at[0]
    pland, eland = proj.at[1], back.at[1]
    for i in range(n_ctx + 1):
        if i < n_ctx:
            s = source(i)
            value = None
            for p in range(PIECES):
                if i > 0:
                    att_copy(s, p, True).wait_recv()
                    chain_each(i, s, lambda right, s=s, p=p: att_copy(s, p, right).start())
                term = jnp.dot(
                    att[s, p],
                    wo[p * piece_width : (p + 1) * piece_width, :],
                    preferred_element_type=f32,
                )
                value = term if value is None else value + term
            part[i] = value.astype(bf16).reshape(part.shape[1:])
            for step in range(1, n_head):
                to_head_owner(i, step).start()
        if i >= 1:
            value = part[i - 1, h].astype(f32)
            for step in range(1, n_head):
                to_head_owner(i - 1, step).wait_recv()
                value = value + part_in[i - 1, step - 1].astype(f32)
            psum[i - 1] = value.astype(bf16)
            if i >= 2:
                to_owner(psum, pland, pz_s, pz_r, i - 1, 1).start()

    def landed(dst, own_sum, send, recv, s):
        return to_ctx(own_sum.at[0], dst.at[s], send.at[0], recv.at[s], (z + 1) % n_ctx)

    loads[6].wait()
    loads[7].wait()
    pland[z] = psum[0]
    for i in range(1, n_ctx):
        landed(pland, psum, pz_s, pz_r, source(i)).wait_recv()
    squares = jnp.zeros((own, 1), f32)
    for s in range(n_ctx):
        columns = slice(s * block, (s + 1) * block)
        value = (pland[s].astype(f32) + res_ref[:, columns].astype(f32)).astype(bf16)
        mixed_ref[:, columns] = value
        value = value.astype(f32)
        squares = squares + jnp.sum(value * value, axis=-1, keepdims=True)
    factor = lax.rsqrt(squares / model + 1e-06)
    tok[z, h, :, :model] = (mixed_ref[...].astype(f32) * factor * gain_ref[...]).astype(bf16)

    def tok_z(s, go_right):
        return chain(tok.at[s, h], tz_s.at[s], tz_r.at[s], s, go_right)

    def tok_x(s):
        return to_head(tok.at[s, h], tok.at[s, h], tx_s.at[s], tx_r.at[s], x_peer)

    def tok_c(s, which):
        b = h if which == 0 else x_peer
        return to_head(tok.at[s, b], tok.at[s, b], tc_s.at[s, which], tc_r.at[s, which], core_peer)

    for load in loads[8:]:
        load.wait()
    tile = 256
    expert = z * lax.axis_size("head") + h

    def hidden_of(s):
        tokens = tok[s, :, :, :model].reshape(4 * own, model)
        table = tok[s, :, :, model:].reshape(4 * own, LANES).astype(f32)
        at = lax.broadcasted_iota(jnp.int32, table.shape, 1)
        weight = jnp.sum(jnp.where(at % half == expert, table, 0.0), axis=-1, keepdims=True)
        acts = []
        for t in range(hidden // tile):
            columns = slice(t * tile, (t + 1) * tile)
            gate_act = jnp.dot(tokens, wg[:, columns], preferred_element_type=f32)
            up_act = jnp.dot(tokens, wu[:, columns], preferred_element_type=f32)
            acts.append((gate_act * (up_act / (1.0 + jnp.exp(-gate_act)))).astype(bf16))
        return jnp.concatenate(acts, axis=1), weight

    width = model // CUT
    wide = min(512, width)

    def output_of(i, hid, weight):
        first = (i % CUT) * width

        for t in range(width // wide):
            columns = slice(t * wide, (t + 1) * wide)
            value = jnp.dot(
                hid,
                wd[:, first + t * wide : first + (t + 1) * wide],
                preferred_element_type=f32,
            )
            store_chunk(epart, i, columns, value.astype(bf16).astype(f32) * weight)

        swap_core(epart, epart_in, ea_s, ea_r, i).start()

    def experts_core(i):
        after_core(i, epart, epart_in, ecross, ea_s, ea_r, ecross_in, ex_s, ex_r)

    def experts_x(i):
        after_x(
            i, epart, epart_in, ecross_in, ecross, ex_s, ex_r, eland, esum, ez_s, ez_r, CUT
        )

    for i in range(n_ctx + 2):
        if i < n_ctx:
            s = source(i)
            if i > 0:
                tok_z(s, True).wait_recv()
            chain_each(i, s, lambda right, s=s: tok_z(s, right).start())
            tok_x(s).start()
            tok_c(s, 0).start()
        if 1 <= i <= n_ctx:
            s = source(i - 1)
            tok_x(s).wait_recv()
            tok_c(s, 1).start()
            tok_c(s, 0).wait_recv()
            tok_c(s, 1).wait_recv()
            hid, weight = hidden_of(s)
        if i >= 2:
            for c in range(CUT):
                experts_core((i - 2) * CUT + c)
        for c in range(CUT):
            if 1 <= i <= n_ctx:
                output_of((i - 1) * CUT + c, hid, weight)
            if i >= 2:
                experts_x((i - 2) * CUT + c)

    for c in range(CUT):
        total = esum[c].astype(f32)
        for i in range(1, n_ctx):
            slot = source(i) * CUT + c
            landed(eland, esum, ez_s, ez_r, slot).wait_recv()
            total = total + eland[slot].astype(f32)
        out_ref[:, c * width : (c + 1) * width] = total.astype(bf16)

    for step in range(1, n_ctx):

        @pl.when(z + step <= last)
        def _():
            kv_copy(z, step).wait_send()

    for i in range(n_ctx):
        s = source(i)
        for p in range(PIECES):
            chain_each(i, s, lambda right, s=s, p=p: att_copy(s, p, right).wait_send())
        chain_each(i, s, lambda right, s=s: tok_z(s, right).wait_send())
        tok_x(s).wait_send()
        tok_c(s, 0).wait_send()
        tok_c(s, 1).wait_send()
        for step in range(1, n_head):
            to_head_owner(i, step).wait_send()
        if i > 0:
            to_owner(psum, pland, pz_s, pz_r, i, 1).wait_send()
    for i in range(n_ctx * CUT):
        swap_core(epart, epart_in, ea_s, ea_r, i).wait_send()
        swap_x(ecross, ecross_in, ex_s, ex_r, i).wait_send()
        if i >= CUT:
            to_owner(esum, eland, ez_s, ez_r, i, CUT).wait_send()


def fused(query, keys, values, residual, o_weight, gain, routes, gates, w_gate, w_up, w_down):
    n, heads = lax.axis_size("ctx"), lax.axis_size("head")
    rows, width = query.shape
    own, model = residual.shape
    hidden = w_gate.shape[2]
    block = o_weight.shape[1]
    bf16 = jnp.bfloat16
    vmem = pl.BlockSpec(memory_space=pltpu.VMEM)
    hbm = pl.BlockSpec(memory_space=pltpu.HBM)
    dma = pltpu.SemaphoreType.DMA

    def sums(slots, columns):
        return [
            pltpu.VMEM((slots, 2, 2, own, columns), bf16),
            pltpu.VMEM((slots, 2, own, columns), bf16),
            pltpu.VMEM((slots, own, columns), bf16),
            pltpu.VMEM((slots, own, columns), bf16),
            pltpu.VMEM((2, slots, own, columns), bf16),
        ]

    flops = 2 * rows * (width * model // 1 + 2 * n * rows * width) + 24 * n * rows * model * hidden // 4
    return pl.pallas_call(
        lambda *refs: layer_kernel(n, *refs),
        out_shape=(
            jax.ShapeDtypeStruct(residual.shape, bf16),
            jax.ShapeDtypeStruct(residual.shape, bf16),
        ),
        in_specs=[hbm] * 11,
        out_specs=(vmem, vmem),
        scratch_shapes=[
            pltpu.VMEM(query.shape, bf16),
            pltpu.VMEM(residual.shape, bf16),
            pltpu.VMEM((1, model), jnp.float32),
            pltpu.VMEM(routes.shape[::-1], jnp.int32),
            pltpu.VMEM(gates.shape[::-1], jnp.float32),
            pltpu.VMEM(o_weight.shape, bf16),
            pltpu.VMEM(w_gate.shape[1:], bf16),
            pltpu.VMEM(w_up.shape[1:], bf16),
            pltpu.VMEM(w_down.shape[1:], bf16),
            pltpu.VMEM((n, 2, rows, HEAD_DIMENSION), bf16),
            pltpu.VMEM((n, PIECES, rows, width // PIECES), bf16),
            pltpu.VMEM((n, heads, own, block), bf16),
            pltpu.VMEM((n, heads - 1, own, block), bf16),
            pltpu.VMEM((2, n, own, block), bf16),
            pltpu.VMEM((n, 4, own, model + LANES), bf16),
            *sums(n * CUT, model // CUT),
            dma((11,)),
            dma((n,)), dma((n,)),
            dma((n, PIECES, 2)), dma((n, PIECES)),
            dma((n, heads - 1)), dma((n, heads - 1)), dma((n,)), dma((n,)),
            dma((n, 2)), dma((n,)), dma((n,)), dma((n,)), dma((n, 2)), dma((n, 2)),
            *[dma((n * CUT,))] * 6,
        ],
        compiler_params=pltpu.CompilerParams(
            collective_id=0, has_side_effects=True, vmem_limit_bytes=44 * 1024 * 1024
        ),
        cost_estimate=pl.CostEstimate(
            flops=flops, bytes_accessed=6 * model * hidden + 2 * width * block, transcendentals=0
        ),
        name="layer",
    )(
        query, keys, values, residual, o_weight, gain.reshape(1, -1), routes.T, gates.T,
        w_gate, w_up, w_down,
    )


def every_token_fits(mesh, *args):
    devices = mesh.shape["ctx"] * mesh.shape["head"]
    own = args[3].shape[0] // (devices * mesh.shape["group"])
    top = args[6].shape[1]
    capacity = min(own, max(2, 2 * own * top // devices))
    return (
        capacity == own
        and mesh.shape["head"] == 4
        and mesh.shape["ctx"] <= 8
        and args[8].shape[0] == devices
        and devices <= LANES // 2
        and own % 16 == 0
        and args[1].shape[1] == 4 * HEAD_DIMENSION
    )


def solution(mesh):
    def run(*args):
        inner = fused if every_token_fits(mesh, *args) else body
        return split(mesh, inner)(*args)

    return run


def split(mesh, inner):
    return jax.shard_map(
        inner,
        mesh=mesh,
        in_specs=(
            P(("group", "ctx"), "head"),
            P(("group", "ctx"), "head"),
            P(("group", "ctx"), "head"),
            P(("group", "ctx", "head"), None),
            P("head", "ctx"),
            P(),
            P(("group", "ctx", "head"), None),
            P(("group", "ctx", "head"), None),
            P(("ctx", "head"), None, None),
            P(("ctx", "head"), None, None),
            P(("ctx", "head"), None, None),
        ),
        out_specs=(P(("group", "ctx", "head"), None), P(("group", "ctx", "head"), None)),
        check_vma=False,
    )
```

```python
import jax
import jax.numpy as jnp
from jax import lax
from jax.experimental import pallas as pl
from jax.experimental.pallas import tpu as pltpu
from jax.sharding import PartitionSpec as P

HEAD_DIMENSION = 128


def expert_apply(arrived, gate_proj, up_proj, down_proj):
    shape_in = arrived.shape
    flat_rows = arrived.reshape(-1, shape_in[-1])
    gate_act = jnp.dot(flat_rows, gate_proj, preferred_element_type=jnp.float32)
    up_act = jnp.dot(flat_rows, up_proj, preferred_element_type=jnp.float32)
    hidden = (jax.nn.silu(gate_act) * up_act).astype(jnp.bfloat16)
    output = jnp.dot(hidden, down_proj, preferred_element_type=jnp.float32).astype(jnp.bfloat16)
    return output.reshape(shape_in)


def body(query, keys, values, residual, o_weight, gain, routes, gates, w_gate, w_up, w_down):
    head_size = HEAD_DIMENSION
    query_rows = query.shape[0]
    kv_heads = keys.shape[1] // head_size
    q_heads = query.shape[1] // head_size
    head_replicas = q_heads // kv_heads
    scale = head_size ** (-0.5)
    queries = query.reshape(query_rows, kv_heads, head_replicas, head_size)
    first_pos = lax.axis_index("ctx") * query_rows
    query_pos = first_pos + jnp.arange(query_rows, dtype=jnp.int32)
    last_pos = first_pos + query_rows - 1

    def accumulate(carry, pieces):
        run_max, run_sum, run_acc = carry
        key_piece, value_piece = pieces
        width = key_piece.shape[0]
        key_pos = jnp.arange(width, dtype=jnp.int32)
        visible = key_pos[None, :] <= query_pos[:, None]
        scores = (
            jnp.einsum(
                "veqi,zei->eqvz",
                queries,
                key_piece.reshape(width, kv_heads, head_size),
                preferred_element_type=jnp.float32,
            )
            * scale
        )
        scores = jnp.where(visible, scores, -1e30)
        new_max = jnp.maximum(run_max, jnp.max(scores, axis=-1))
        weights = jnp.where(visible, jnp.exp(scores - new_max[..., None]), 0.0)
        new_sum = jnp.sum(weights, axis=-1)
        update = jnp.einsum(
            "pexa,apo->pexo",
            weights.astype(jnp.bfloat16),
            value_piece.reshape(width, kv_heads, head_size),
            preferred_element_type=jnp.float32,
        )
        return (new_max, new_sum, update)

    start_state = (
        jnp.full((kv_heads, head_replicas, query_rows), -1e30, jnp.float32),
        jnp.zeros((kv_heads, head_replicas, query_rows), jnp.float32),
        jnp.zeros((kv_heads, head_replicas, query_rows, head_size), jnp.float32),
    )
    pieces = (
        lax.all_gather(keys, "ctx", axis=0, tiled=True),
        lax.all_gather(values, "ctx", axis=0, tiled=True),
    )
    run_max, run_sum, run_acc = lax.cond(
        jnp.int32(0) > last_pos, lambda: start_state, lambda: accumulate(start_state, pieces)
    )
    attended = (
        (run_acc / run_sum[..., None])
        .transpose(2, 0, 1, 3)
        .reshape(query_rows, q_heads * head_size)
        .astype(jnp.bfloat16)
    )
    head_terms = jnp.dot(
        attended,
        lax.all_gather(o_weight, "ctx", axis=1, tiled=True),
        preferred_element_type=jnp.float32,
    )
    summed = lax.psum_scatter(
        head_terms.astype(jnp.bfloat16), "head", scatter_dimension=0, tiled=True
    ).astype(jnp.float32)
    mixed = (summed + residual.astype(jnp.float32)).astype(jnp.bfloat16)
    mixed_f = mixed.astype(jnp.float32)
    normed = (
        mixed_f * lax.rsqrt(jnp.mean(mixed_f * mixed_f, axis=-1, keepdims=True) + 1e-06) * gain
    ).astype(jnp.bfloat16)
    own_rows = residual.shape[0]
    model_dim = residual.shape[1]
    top_count = routes.shape[1]
    ctx_count = lax.axis_size("ctx")
    head_count = lax.axis_size("head")
    devices = ctx_count * head_count
    capacity = min(own_rows, max(2, 2 * own_rows * top_count // devices))
    expert_ids = routes.reshape(-1)
    onehot = (expert_ids[:, None] == jnp.arange(devices, dtype=jnp.int32)[None, :]).astype(
        jnp.int32
    )
    slots = jnp.sum((jnp.cumsum(onehot, axis=0) - 1) * onehot, axis=1)
    target = expert_ids * capacity + slots
    outgoing = (
        jnp.zeros((devices * capacity, model_dim), jnp.bfloat16)
        .at[target]
        .set(jnp.repeat(normed, top_count, axis=0))
    )
    outgoing = outgoing.reshape(devices, capacity, model_dim)
    gate_proj = w_gate[0]
    up_proj = w_up[0]
    down_proj = w_down[0]
    computed = expert_apply(
        lax.all_to_all(outgoing, ("ctx", "head"), split_axis=0, concat_axis=0, tiled=True),
        gate_proj,
        up_proj,
        down_proj,
    )
    returned = lax.all_to_all(computed, ("ctx", "head"), split_axis=0, concat_axis=0, tiled=True)
    selected_entries = returned.reshape(devices * capacity, model_dim)[target]
    selected_entries = selected_entries.astype(jnp.float32).reshape(own_rows, top_count, model_dim)
    weight_norm = gates / jnp.sum(gates, axis=-1, keepdims=True)
    expert_mix = jnp.sum(selected_entries * weight_norm[..., None], axis=1).astype(jnp.bfloat16)
    return (mixed, expert_mix)


LANES = 128
PIECES = 2
CUT = 2
MESH = pl.DeviceIdType.MESH


def layer_kernel(
    n_ctx,
    q_hbm, k_hbm, v_hbm, res_hbm, wo_hbm, gain_hbm, routes_hbm, gates_hbm, wg_hbm, wu_hbm, wd_hbm,
    mixed_ref, out_ref,
    q_ref, res_ref, gain_ref, routes_ref, gates_ref, wo, wg, wu, wd,
    kv, att, part, part_in, proj,
    tok, epart, epart_in, ecross, ecross_in, back,
    local_sem,
    kv_s, kv_r, att_s, att_r, pa_s, pa_r, pz_s, pz_r,
    tz_s, tz_r, tx_s, tx_r, tc_s, tc_r, ea_s, ea_r, ex_s, ex_r, ez_s, ez_r,
):
    f32, bf16 = jnp.float32, jnp.bfloat16
    z = lax.axis_index("ctx")
    h = lax.axis_index("head")
    x, core = h // 2, h % 2
    core_peer = x * 2 + (1 - core)
    x_peer = (1 - x) * 2 + core
    rows, own, model = q_ref.shape[0], res_ref.shape[0], res_ref.shape[1]
    size = HEAD_DIMENSION
    q_heads = q_ref.shape[1] // size
    piece_heads = q_heads // PIECES
    piece_width = piece_heads * size
    block = model // n_ctx
    hidden = wg.shape[1]

    loads = [
        pltpu.make_async_copy(src, dst, local_sem.at[i])
        for i, (src, dst) in enumerate(
            (
                (k_hbm, kv.at[z, 0]),
                (v_hbm, kv.at[z, 1]),
                (routes_hbm, routes_ref),
                (gates_hbm, gates_ref),
                (q_hbm, q_ref),
                (wo_hbm, wo),
                (res_hbm, res_ref),
                (gain_hbm, gain_ref),
                (wg_hbm.at[0], wg),
                (wu_hbm.at[0], wu),
                (wd_hbm.at[0], wd),
            )
        )
    ]
    for load in loads:
        load.start()

    barrier = pltpu.get_barrier_semaphore()
    n_head = lax.axis_size("head")
    for step in range(1, n_head):
        pl.semaphore_signal(
            barrier, inc=1, device_id={"head": (h + step) % n_head}, device_id_type=MESH
        )
    for step in range(1, n_ctx):
        pl.semaphore_signal(
            barrier, inc=1, device_id={"ctx": (z + step) % n_ctx}, device_id_type=MESH
        )

    for other in range(1, n_ctx):

        @pl.when(z < other)
        def _():
            kv[other] = jnp.zeros(kv.shape[1:], bf16)

    loads[2].wait()
    loads[3].wait()
    gate_values = gates_ref[...].T
    gate_norm = gate_values / jnp.sum(gate_values, axis=-1, keepdims=True)
    route_values = routes_ref[...].T
    lane = lax.broadcasted_iota(jnp.int32, (own, LANES), 1)
    half = LANES // 2
    table = jnp.zeros((own, LANES), f32)
    for k in range(route_values.shape[1]):
        table = table + jnp.where(
            lane % half == route_values[:, k : k + 1], gate_norm[:, k : k + 1], 0.0
        )
    high = table.astype(bf16).astype(f32)
    tok[z, h, :, model:] = jnp.where(lane < half, high, table - high).astype(bf16)

    pl.semaphore_wait(barrier, n_ctx + n_head - 2)

    def to_ctx(src, dst, send, recv, target):
        return pltpu.make_async_remote_copy(
            src_ref=src, dst_ref=dst, send_sem=send, recv_sem=recv,
            device_id={"ctx": target}, device_id_type=MESH,
        )

    def to_head(src, dst, send, recv, target):
        return pltpu.make_async_remote_copy(
            src_ref=src, dst_ref=dst, send_sem=send, recv_sem=recv,
            device_id={"head": target}, device_id_type=MESH,
        )

    last = n_ctx - 1
    short = jnp.minimum(z, last - z)
    toward = jnp.where(z * 2 < last, -1, 1)

    def source(i):
        if i == 0:
            return z
        near = toward * ((i + 1) // 2) if i % 2 else -toward * (i // 2)
        return z + jnp.where(i <= 2 * short, near, -toward * (i - short))

    def kv_copy(s, step):
        return to_ctx(
            kv.at[s], kv.at[s], kv_s.at[step], kv_r.at[s], jnp.minimum(z + step, last)
        )

    loads[0].wait()
    loads[1].wait()
    for step in range(1, n_ctx):

        @pl.when(z + step <= last)
        def _():
            kv_copy(z, step).start()

    loads[4].wait()
    for step in range(1, n_ctx):

        @pl.when(z >= step)
        def _():
            kv_copy(z - step, step).wait_recv()

    def chain(buf_at, send, recv, s, go_right):
        way = 1 if go_right else 0
        target = jnp.clip(z + (1 if go_right else -1), 0, last)
        return to_ctx(buf_at, buf_at, send.at[way], recv, target)

    def chain_each(i, s, run):
        @pl.when((s <= z) & (z < last))
        def _():
            run(True)

        @pl.when((s >= z) & (z > 0))
        def _():
            run(False)

    def att_copy(s, p, go_right):
        return chain(att.at[s, p], att_s.at[s, p], att_r.at[s, p], s, go_right)

    keys_all = kv[:, 0].reshape(n_ctx * rows, size)
    values_all = kv[:, 1].reshape(n_ctx * rows, size)
    row_at = lax.broadcasted_iota(jnp.int32, (rows, n_ctx * rows), 0)
    col_at = lax.broadcasted_iota(jnp.int32, (rows, n_ctx * rows), 1)
    visible = col_at <= row_at + z * rows
    scale = size ** (-0.5)
    for p in range(PIECES):
        for j in range(piece_heads):
            head = p * piece_heads + j
            scores = lax.dot_general(
                q_ref[:, head * size : (head + 1) * size],
                keys_all,
                (((1,), (1,)), ((), ())),
                preferred_element_type=f32,
            )
            scores = jnp.where(visible, scores * scale, -1e30)
            top = jnp.max(scores, axis=-1, keepdims=True)
            weights = jnp.exp(scores - top)
            total = jnp.sum(weights, axis=-1, keepdims=True)
            summed = jnp.dot(weights.astype(bf16), values_all, preferred_element_type=f32)
            att[z, p, :, j * size : (j + 1) * size] = (summed / total).astype(bf16)
        chain_each(0, z, lambda right, p=p: att_copy(z, p, right).start())

    def swap_core(buf, buf_in, send, recv, i):
        return to_head(buf.at[i, 1 - core], buf_in.at[i], send.at[i], recv.at[i], core_peer)

    def swap_x(buf, buf_in, send, recv, i):
        return to_head(buf.at[i], buf_in.at[i], send.at[i], recv.at[i], x_peer)

    def to_owner(buf, dst, send, recv, i, cut):
        slot = z * cut + i % cut
        return to_ctx(buf.at[i], dst.at[slot], send.at[i], recv.at[slot], source(i // cut))

    def to_head_owner(i, step):
        peer = (h + step) % n_head
        return to_head(
            part.at[i, peer], part_in.at[i, step - 1],
            pa_s.at[i, step - 1], pa_r.at[i, step - 1], peer,
        )

    def store_chunk(buf, i, columns, value):
        parts = value.astype(bf16).reshape(2, 2, own, value.shape[-1])
        for cc in range(2):
            for xx in range(2):
                buf[i, cc, xx, :, columns] = parts[xx, cc]

    def after_core(i, buf, buf_in, crossed, a_s, a_r, crossed_in, x_s, x_r):
        swap_core(buf, buf_in, a_s, a_r, i).wait_recv()
        crossed[i] = (
            buf[i, core, 1 - x].astype(f32) + buf_in[i, 1 - x].astype(f32)
        ).astype(bf16)
        swap_x(crossed, crossed_in, x_s, x_r, i).start()

    def after_x(i, buf, buf_in, crossed_in, crossed, x_s, x_r, dst, own_sum, z_s, z_r, cut):
        swap_x(crossed, crossed_in, x_s, x_r, i).wait_recv()
        value = (
            buf[i, core, x].astype(f32)
            + buf_in[i, x].astype(f32)
            + crossed_in[i].astype(f32)
        ).astype(bf16)
        own_sum[i] = value
        if i >= cut:
            to_owner(own_sum, dst, z_s, z_r, i, cut).start()

    loads[5].wait()
    psum, esum = proj.at[0], back.at[0]
    pland, eland = proj.at[1], back.at[1]
    for i in range(n_ctx + 1):
        if i < n_ctx:
            s = source(i)
            value = None
            for p in range(PIECES):
                if i > 0:
                    att_copy(s, p, True).wait_recv()
                    chain_each(i, s, lambda right, s=s, p=p: att_copy(s, p, right).start())
                term = jnp.dot(
                    att[s, p],
                    wo[p * piece_width : (p + 1) * piece_width, :],
                    preferred_element_type=f32,
                )
                value = term if value is None else value + term
            part[i] = value.astype(bf16).reshape(part.shape[1:])
            for step in range(1, n_head):
                to_head_owner(i, step).start()
        if i >= 1:
            value = part[i - 1, h].astype(f32)
            for step in range(1, n_head):
                to_head_owner(i - 1, step).wait_recv()
                value = value + part_in[i - 1, step - 1].astype(f32)
            psum[i - 1] = value.astype(bf16)
            if i >= 2:
                to_owner(psum, pland, pz_s, pz_r, i - 1, 1).start()

    def landed(dst, own_sum, send, recv, s):
        return to_ctx(own_sum.at[0], dst.at[s], send.at[0], recv.at[s], (z + 1) % n_ctx)

    loads[6].wait()
    loads[7].wait()
    pland[z] = psum[0]
    for i in range(1, n_ctx):
        landed(pland, psum, pz_s, pz_r, source(i)).wait_recv()
    squares = jnp.zeros((own, 1), f32)
    for s in range(n_ctx):
        columns = slice(s * block, (s + 1) * block)
        value = (pland[s].astype(f32) + res_ref[:, columns].astype(f32)).astype(bf16)
        mixed_ref[:, columns] = value
        value = value.astype(f32)
        squares = squares + jnp.sum(value * value, axis=-1, keepdims=True)
    factor = lax.rsqrt(squares / model + 1e-06)
    tok[z, h, :, :model] = (mixed_ref[...].astype(f32) * factor * gain_ref[...]).astype(bf16)

    def tok_z(s, go_right):
        return chain(tok.at[s, h], tz_s.at[s], tz_r.at[s], s, go_right)

    def tok_x(s):
        return to_head(tok.at[s, h], tok.at[s, h], tx_s.at[s], tx_r.at[s], x_peer)

    def tok_c(s, which):
        b = h if which == 0 else x_peer
        return to_head(tok.at[s, b], tok.at[s, b], tc_s.at[s, which], tc_r.at[s, which], core_peer)

    for load in loads[8:]:
        load.wait()
    tile = 256
    expert = z * lax.axis_size("head") + h

    def hidden_of(s):
        tokens = tok[s, :, :, :model].reshape(4 * own, model)
        table = tok[s, :, :, model:].reshape(4 * own, LANES).astype(f32)
        at = lax.broadcasted_iota(jnp.int32, table.shape, 1)
        weight = jnp.sum(jnp.where(at % half == expert, table, 0.0), axis=-1, keepdims=True)
        acts = []
        for t in range(hidden // tile):
            columns = slice(t * tile, (t + 1) * tile)
            gate_act = jnp.dot(tokens, wg[:, columns], preferred_element_type=f32)
            up_act = jnp.dot(tokens, wu[:, columns], preferred_element_type=f32)
            acts.append((gate_act * (up_act / (1.0 + jnp.exp(-gate_act)))).astype(bf16))
        return jnp.concatenate(acts, axis=1), weight

    width = model // CUT
    wide = min(512, width)

    def output_of(i, hid, weight):
        first = (i % CUT) * width

        for t in range(width // wide):
            columns = slice(t * wide, (t + 1) * wide)
            value = jnp.dot(
                hid,
                wd[:, first + t * wide : first + (t + 1) * wide],
                preferred_element_type=f32,
            )
            store_chunk(epart, i, columns, value.astype(bf16).astype(f32) * weight)

        swap_core(epart, epart_in, ea_s, ea_r, i).start()

    def experts_core(i):
        after_core(i, epart, epart_in, ecross, ea_s, ea_r, ecross_in, ex_s, ex_r)

    def experts_x(i):
        after_x(
            i, epart, epart_in, ecross_in, ecross, ex_s, ex_r, eland, esum, ez_s, ez_r, CUT
        )

    def spread(i):
        s = source(i)
        if i > 0:
            tok_z(s, True).wait_recv()
        chain_each(i, s, lambda right, s=s: tok_z(s, right).start())
        tok_x(s).start()
        tok_c(s, 0).start()

    def crossed_tokens(i):
        s = source(i)
        tok_x(s).wait_recv()
        tok_c(s, 1).start()

    order = [*range(1, n_ctx), 0]
    spread(0)
    spread(1)
    crossed_tokens(order[0])
    for i in range(2, min(3, n_ctx)):
        spread(i)
    before = None
    for turn, i in enumerate(order):
        s = source(i)
        tok_c(s, 0).wait_recv()
        tok_c(s, 1).wait_recv()
        hid, weight = hidden_of(s)
        if turn + 3 < n_ctx:
            spread(turn + 3)
        if turn + 1 < n_ctx:
            crossed_tokens(order[turn + 1])
        for c in range(CUT):
            if before is not None:
                experts_core(before * CUT + c)
        for c in range(CUT):
            output_of(i * CUT + c, hid, weight)
            if before is not None:
                experts_x(before * CUT + c)
        before = i
    for c in range(CUT):
        experts_core(before * CUT + c)
    for c in range(CUT):
        experts_x(before * CUT + c)

    for c in range(CUT):
        total = esum[c].astype(f32)
        for i in range(1, n_ctx):
            slot = source(i) * CUT + c
            landed(eland, esum, ez_s, ez_r, slot).wait_recv()
            total = total + eland[slot].astype(f32)
        out_ref[:, c * width : (c + 1) * width] = total.astype(bf16)

    for step in range(1, n_ctx):

        @pl.when(z + step <= last)
        def _():
            kv_copy(z, step).wait_send()

    for i in range(n_ctx):
        s = source(i)
        for p in range(PIECES):
            chain_each(i, s, lambda right, s=s, p=p: att_copy(s, p, right).wait_send())
        chain_each(i, s, lambda right, s=s: tok_z(s, right).wait_send())
        tok_x(s).wait_send()
        tok_c(s, 0).wait_send()
        tok_c(s, 1).wait_send()
        for step in range(1, n_head):
            to_head_owner(i, step).wait_send()
        if i > 0:
            to_owner(psum, pland, pz_s, pz_r, i, 1).wait_send()
    for i in range(n_ctx * CUT):
        swap_core(epart, epart_in, ea_s, ea_r, i).wait_send()
        swap_x(ecross, ecross_in, ex_s, ex_r, i).wait_send()
        if i >= CUT:
            to_owner(esum, eland, ez_s, ez_r, i, CUT).wait_send()


def fused(query, keys, values, residual, o_weight, gain, routes, gates, w_gate, w_up, w_down):
    n, heads = lax.axis_size("ctx"), lax.axis_size("head")
    rows, width = query.shape
    own, model = residual.shape
    hidden = w_gate.shape[2]
    block = o_weight.shape[1]
    bf16 = jnp.bfloat16
    vmem = pl.BlockSpec(memory_space=pltpu.VMEM)
    hbm = pl.BlockSpec(memory_space=pltpu.HBM)
    dma = pltpu.SemaphoreType.DMA

    def sums(slots, columns):
        return [
            pltpu.VMEM((slots, 2, 2, own, columns), bf16),
            pltpu.VMEM((slots, 2, own, columns), bf16),
            pltpu.VMEM((slots, own, columns), bf16),
            pltpu.VMEM((slots, own, columns), bf16),
            pltpu.VMEM((2, slots, own, columns), bf16),
        ]

    flops = 2 * rows * (width * model // 1 + 2 * n * rows * width) + 24 * n * rows * model * hidden // 4
    return pl.pallas_call(
        lambda *refs: layer_kernel(n, *refs),
        out_shape=(
            jax.ShapeDtypeStruct(residual.shape, bf16),
            jax.ShapeDtypeStruct(residual.shape, bf16),
        ),
        in_specs=[hbm] * 11,
        out_specs=(vmem, vmem),
        scratch_shapes=[
            pltpu.VMEM(query.shape, bf16),
            pltpu.VMEM(residual.shape, bf16),
            pltpu.VMEM((1, model), jnp.float32),
            pltpu.VMEM(routes.shape[::-1], jnp.int32),
            pltpu.VMEM(gates.shape[::-1], jnp.float32),
            pltpu.VMEM(o_weight.shape, bf16),
            pltpu.VMEM(w_gate.shape[1:], bf16),
            pltpu.VMEM(w_up.shape[1:], bf16),
            pltpu.VMEM(w_down.shape[1:], bf16),
            pltpu.VMEM((n, 2, rows, HEAD_DIMENSION), bf16),
            pltpu.VMEM((n, PIECES, rows, width // PIECES), bf16),
            pltpu.VMEM((n, heads, own, block), bf16),
            pltpu.VMEM((n, heads - 1, own, block), bf16),
            pltpu.VMEM((2, n, own, block), bf16),
            pltpu.VMEM((n, 4, own, model + LANES), bf16),
            *sums(n * CUT, model // CUT),
            dma((11,)),
            dma((n,)), dma((n,)),
            dma((n, PIECES, 2)), dma((n, PIECES)),
            dma((n, heads - 1)), dma((n, heads - 1)), dma((n,)), dma((n,)),
            dma((n, 2)), dma((n,)), dma((n,)), dma((n,)), dma((n, 2)), dma((n, 2)),
            *[dma((n * CUT,))] * 6,
        ],
        compiler_params=pltpu.CompilerParams(
            collective_id=0, has_side_effects=True, vmem_limit_bytes=56 * 1024 * 1024
        ),
        cost_estimate=pl.CostEstimate(
            flops=flops, bytes_accessed=6 * model * hidden + 2 * width * block, transcendentals=0
        ),
        name="layer",
    )(
        query, keys, values, residual, o_weight, gain.reshape(1, -1), routes.T, gates.T,
        w_gate, w_up, w_down,
    )


def every_token_fits(mesh, *args):
    devices = mesh.shape["ctx"] * mesh.shape["head"]
    own = args[3].shape[0] // (devices * mesh.shape["group"])
    top = args[6].shape[1]
    capacity = min(own, max(2, 2 * own * top // devices))
    return (
        capacity == own
        and mesh.shape["head"] == 4
        and 2 <= mesh.shape["ctx"] <= 8
        and args[8].shape[0] == devices
        and devices <= LANES // 2
        and own % 16 == 0
        and args[1].shape[1] == 4 * HEAD_DIMENSION
    )


def solution(mesh):
    def run(*args):
        inner = fused if every_token_fits(mesh, *args) else body
        return split(mesh, inner)(*args)

    return run


def split(mesh, inner):
    return jax.shard_map(
        inner,
        mesh=mesh,
        in_specs=(
            P(("group", "ctx"), "head"),
            P(("group", "ctx"), "head"),
            P(("group", "ctx"), "head"),
            P(("group", "ctx", "head"), None),
            P("head", "ctx"),
            P(),
            P(("group", "ctx", "head"), None),
            P(("group", "ctx", "head"), None),
            P(("ctx", "head"), None, None),
            P(("ctx", "head"), None, None),
            P(("ctx", "head"), None, None),
        ),
        out_specs=(P(("group", "ctx", "head"), None), P(("group", "ctx", "head"), None)),
        check_vma=False,
    )
```
